32 devices in a mesh: sub: 16 (over z, y, x), crs: 2 (over core).
Axes of the slice: x: 2, y: 2, z: 4, core: 2. Of those that a mesh axis runs over, the one named last changes fastest.
Arguments:
- right_side: float32 [4, 16, 2, 384], P(None, 'sub', 'crs'), may hold values from -40 to 40
- own_block: bfloat16 [16, 2, 384, 384], P('sub', 'crs'), may hold values from -1 to 3
- coupling: bfloat16 [16, 2, 384, 768], P('sub', 'crs'), may hold values from -0.1875 to 0.1875
- local_inverse: bfloat16 [16, 2, 384, 1152], P('sub', 'crs'), may hold values from -1 to 3
- coarse_basis: float32 [16, 2, 40, 384], P('sub', 'crs'), may hold values from -0.3125 to 0.3125
- coarse_inverse: bfloat16 [16, 80, 2, 640], P('sub', None, 'crs'), may hold values from -1 to 4
- neighbours: int32 [16, 2, 6], P('sub', 'crs'), may hold values from 0 to 15, as said below
- margin_rows: int32 [16, 2, 6, 128], P('sub', 'crs'), may hold values from 0 to 383, as said below
- block_counts: int32 [16, 2], P('sub', 'crs'), may hold values from 4 to 6, as said below
Outputs:
- solution: float32 [4, 16, 2, 384], P(None, 'sub', 'crs')
- basis_next: float32 [4, 16, 2, 384], P(None, 'sub', 'crs')
The draws below stay inside these ranges and needn't reach their ends.
Inputs may be any that keep to these rules, and one draw needn't show every extreme that they name: A subdomain's listed neighbours are distinct sub indices other than its own; slot j of (s, c) names subdomain (neighbours[s, c, j], c). `margin_rows`: the rows of one block are distinct. `block_counts`: some subdomain uses all 6 slots.
All inputs are finite; a program needn't handle non-finite values.
Results may differ from the reference program's by a relative error of at most 0.0095.
Values may be sent and summed in bfloat16 or wider, within the bound.
A program may use at most 64 MiB of HBM per device.

```python
import math
import jax
import jax.numpy as jnp
from jax import lax

OWN_ROWS = 384
BLK = 128
NBMAX = 6
KC = 40
COLS = 4
ITERS = 2
SUBS = 16
OWNERS = 2
ROWS_ALL = 12288


def draw_right_side(key, part):
    key = jax.random.fold_in(key, 101)
    key_base, key_scale = jax.random.split(key)
    full_shape = (COLS, SUBS, OWNERS, OWN_ROWS)
    position = (lax.broadcasted_iota(jnp.float32, full_shape, 1) * OWNERS + lax.broadcasted_iota(jnp.float32, full_shape, 2)) / (SUBS * OWNERS - 1)
    row_scale = jnp.exp(jax.random.uniform(key_scale, (1, SUBS, OWNERS, OWN_ROWS), jnp.float32, math.log(0.5), math.log(5.0)))
    trend_scale = 1.0 + 0.8 * position
    values = jnp.clip(jax.random.normal(key_base, full_shape, jnp.float32), -4.0, 4.0)
    return values * row_scale * trend_scale


def draw_own_block(key, part):
    key = jax.random.fold_in(key, 102)
    key_one, key_two = jax.random.split(key)
    full_shape = (SUBS, OWNERS, OWN_ROWS, OWN_ROWS)
    noise_part = jnp.clip(jax.random.normal(key_one, full_shape, jnp.float32), -4.0, 4.0) * (OWN_ROWS + NBMAX * BLK) ** (-0.5)
    diagonal = jax.random.uniform(key_two, (SUBS, OWNERS, OWN_ROWS, 1), jnp.float32, 1.0, 2.0)
    on_diagonal = lax.broadcasted_iota(jnp.int32, full_shape, 2) == lax.broadcasted_iota(jnp.int32, full_shape, 3)
    return (noise_part + jnp.where(on_diagonal, diagonal, 0.0)).astype(jnp.bfloat16)


def draw_local_inverse(key, part):
    key = jax.random.fold_in(key, 103)
    key_one, key_two = jax.random.split(key)
    full_shape = (SUBS, OWNERS, OWN_ROWS, OWN_ROWS + NBMAX * BLK)
    noise_part = jnp.clip(jax.random.normal(key_one, full_shape, jnp.float32), -4.0, 4.0) * (OWN_ROWS + NBMAX * BLK) ** (-0.5)
    diagonal = jax.random.uniform(key_two, (SUBS, OWNERS, OWN_ROWS, 1), jnp.float32, 0.8, 1.6)
    on_diagonal = lax.broadcasted_iota(jnp.int32, full_shape, 2) == lax.broadcasted_iota(jnp.int32, full_shape, 3)
    return (noise_part + jnp.where(on_diagonal, diagonal, 0.0)).astype(jnp.bfloat16)


def draw_coarse_inverse(key, part):
    key = jax.random.fold_in(key, 104)
    full_shape = (SUBS, OWNERS * KC, OWNERS, SUBS * KC)
    noise_part = jnp.clip(jax.random.normal(key, full_shape, jnp.float32), -4.0, 4.0) * (SUBS * OWNERS * KC) ** (-0.5)
    sub_rows = lax.broadcasted_iota(jnp.int32, (SUBS, 1, 1, 1), 0)
    sub_cols = lax.broadcasted_iota(jnp.int32, (1, 1, 1, SUBS * KC), 3)
    owner_rows = lax.broadcasted_iota(jnp.int32, (1, OWNERS * KC, 1, 1), 1)
    owner_cols = lax.broadcasted_iota(jnp.int32, (1, 1, OWNERS, 1), 2)
    matches = (sub_rows == sub_cols // KC) & (owner_rows // KC == owner_cols) & (owner_rows % KC == sub_cols % KC)
    return (noise_part + jnp.where(matches, 3.0, 0.0)).astype(jnp.bfloat16)


def draw_neighbours(key, part):
    key = jax.random.fold_in(key, 105)
    full_shape = (SUBS, OWNERS, SUBS - 1)
    scores = jax.random.randint(key, full_shape, 0, 1 << 20) * (SUBS - 1) + lax.broadcasted_iota(jnp.int32, full_shape, 2)
    ranking = jnp.argsort(scores, axis=2)[:, :, :NBMAX].astype(jnp.int32)
    own_index = lax.broadcasted_iota(jnp.int32, (SUBS, OWNERS, NBMAX), 0)
    return ((own_index + 1 + ranking) % SUBS).astype(jnp.int32)


def draw_margin_rows(key, part):
    key = jax.random.fold_in(key, 106)
    full_shape = (SUBS, OWNERS, NBMAX, OWN_ROWS)
    scores = jax.random.randint(key, full_shape, 0, 1 << 20) * OWN_ROWS + lax.broadcasted_iota(jnp.int32, full_shape, 3)
    return jnp.argsort(scores, axis=3)[:, :, :, :BLK].astype(jnp.int32)


def draw_block_counts(key, part):
    key = jax.random.fold_in(key, 107)
    key_one, key_two = jax.random.split(key)
    counts = NBMAX - 2 + jax.random.randint(key_one, (SUBS, OWNERS), 0, 3)
    forced_index = jax.random.randint(key_two, (), 0, SUBS * OWNERS)
    flat_index = lax.broadcasted_iota(jnp.int32, (SUBS, OWNERS), 0) * OWNERS + lax.broadcasted_iota(jnp.int32, (SUBS, OWNERS), 1)
    return jnp.where(flat_index == forced_index, NBMAX, counts).astype(jnp.int32)


def level_of(key, extent, cuts, least, top_value):
    gain = 1.0
    for axis_at, shards_of in cuts:
        draws = jax.random.uniform(jax.random.fold_in(jax.random.fold_in(key, 6), axis_at), (shards_of,), jnp.float32, least / len(cuts), top_value / len(cuts))
        gain = gain * jnp.repeat(jnp.exp(draws), extent[axis_at] // shards_of).reshape((-1,) + (1,) * (len(extent) - 1 - axis_at))
    return gain


def gaussian(rng, dims, scale, limit, cuts=(), held_as=jnp.bfloat16):
    level = level_of(rng, dims, cuts, -0.22, 0.18) if cuts else 1.0
    drawn = jax.random.normal(rng, dims, jnp.float32) * scale * level
    return jnp.minimum(jnp.maximum(drawn, -limit), limit).astype(held_as)


def setup_inputs(seed: int = 0) -> dict:
    key_of = jax.random.split(jax.random.key(seed), 10)
    return {
        "right_side": draw_right_side(jax.random.fold_in(key_of[9], 71), 0),
        "own_block": draw_own_block(jax.random.fold_in(key_of[9], 71), 0),
        "coupling": gaussian(key_of[2], (SUBS, OWNERS, OWN_ROWS, NBMAX * BLK), (OWN_ROWS + NBMAX * BLK) ** -0.5, 0.1875, ((0, 16), (1, 2))),
        "local_inverse": draw_local_inverse(jax.random.fold_in(key_of[9], 71), 0),
        "coarse_basis": gaussian(key_of[4], (SUBS, OWNERS, KC, OWN_ROWS), OWN_ROWS ** -0.5, 0.3125, ((0, 16), (1, 2)), jnp.float32),
        "coarse_inverse": draw_coarse_inverse(jax.random.fold_in(key_of[9], 71), 0),
        "neighbours": draw_neighbours(jax.random.fold_in(key_of[9], 71), 0),
        "margin_rows": draw_margin_rows(jax.random.fold_in(key_of[9], 71), 0),
        "block_counts": draw_block_counts(jax.random.fold_in(key_of[9], 71), 0),
    }


epsilon = 1e-06

def margin_of(vector_low, neighbours, margin_rows, block_counts):
    subs_here, owners_here, slot_count, block_rows = margin_rows.shape
    owner_index = lax.broadcasted_iota(jnp.int32, margin_rows.shape, 1)
    sub_index = jnp.broadcast_to(neighbours[:, :, :, None], margin_rows.shape).astype(jnp.int32)
    fetched = vector_low[sub_index, owner_index, :, margin_rows.astype(jnp.int32)]
    fetched = jnp.moveaxis(fetched, 4, 2)
    live_slots = jnp.arange(slot_count)[None, None, :] < block_counts[:, :, None]
    fetched = jnp.where(live_slots[:, :, None, :, None], fetched, jnp.zeros_like(fetched))
    return fetched.reshape(subs_here, owners_here, fetched.shape[2], slot_count * block_rows)

def apply_local(matrices, vectors):

    def per_group(members):
        matrix_one, vector_one = members
        return jnp.einsum('crk,cqk->cqr', matrix_one.astype(jnp.float32), vector_one.astype(jnp.float32))
    return lax.map(per_group, (matrices, vectors))

def spread(values):
    return values[None, None, :, None]

def least_squares(start_norm, columns):
    cosines = []
    sine_terms = []
    triangle = []
    target = [start_norm] + [jnp.zeros_like(start_norm) for j in range(len(columns))]
    for j, column in enumerate(columns):
        column = list(column)
        for i in range(j):
            upper_value = cosines[i] * column[i] + sine_terms[i] * column[i + 1]
            column[i + 1] = -sine_terms[i] * column[i] + cosines[i] * column[i + 1]
            column[i] = upper_value
        radius = jnp.sqrt(column[j] * column[j] + column[j + 1] * column[j + 1])
        cosine = column[j] / radius
        sine_part = column[j + 1] / radius
        column[j] = radius
        target[j + 1] = -sine_part * target[j]
        target[j] = cosine * target[j]
        cosines.append(cosine)
        sine_terms.append(sine_part)
        triangle.append(column[:j + 1])
    weights = [None] * len(columns)
    for j in reversed(range(len(columns))):
        running = target[j]
        for k in range(j + 1, len(columns)):
            running = running - triangle[k][j] * weights[k]
        weights[j] = running / triangle[j][j]
    return weights

def reference(right_side, own_block, coupling, local_inverse, coarse_basis, coarse_inverse, neighbours, margin_rows, block_counts):
    right_cols = jnp.transpose(right_side, (1, 2, 0, 3))
    coarse_view = coarse_inverse.reshape(SUBS, OWNERS, KC, OWNERS, SUBS, KC)

    def operate(vector):
        vector_low = vector.astype(jnp.bfloat16)
        margin = margin_of(vector_low, neighbours, margin_rows, block_counts)
        return apply_local(own_block, vector_low) + apply_local(coupling, margin)

    def precondition(vector):
        vector_low = vector.astype(jnp.bfloat16)
        margin = margin_of(vector_low, neighbours, margin_rows, block_counts)
        fine_part = apply_local(local_inverse, jnp.concatenate([vector_low, margin], axis=3))
        restricted = jnp.einsum('sckr,scqr->scqk', coarse_basis, vector, precision=lax.Precision.HIGHEST).astype(jnp.bfloat16)
        restricted_wide = restricted.astype(jnp.float32)

        def solve_rows(matrix):
            return jnp.einsum('akbjl,jbql->aqk', matrix.astype(jnp.float32), restricted_wide)
        solved = lax.map(solve_rows, coarse_view)
        coarse_part = jnp.einsum('scqk,sckr->scqr', solved, coarse_basis, precision=lax.Precision.HIGHEST)
        return fine_part + coarse_part

    def mean_product(first, second):
        return lax.optimization_barrier(jnp.sum(first * second, axis=(0, 1, 3))) / ROWS_ALL
    start_norm = jnp.sqrt(mean_product(right_cols, right_cols) + epsilon)
    krylov = [right_cols / spread(start_norm)]
    directions = []
    columns = []
    for j in range(ITERS):
        direction = precondition(krylov[j])
        mapped = operate(direction)
        heights = [mean_product(mapped, krylov[i]) for i in range(j + 1)]
        for i in range(j + 1):
            mapped = mapped - spread(heights[i]) * krylov[i]
        length = jnp.sqrt(mean_product(mapped, mapped) + epsilon)
        columns.append(heights + [length])
        krylov.append(mapped / spread(length))
        directions.append(direction)
    weights = least_squares(start_norm, columns)
    solution = spread(weights[0]) * directions[0]
    for j in range(1, ITERS):
        solution = solution + spread(weights[j]) * directions[j]
    return (jnp.transpose(solution, (2, 0, 1, 3)), jnp.transpose(krylov[-1], (2, 0, 1, 3)))
```

```python
import functools

import jax
import jax.numpy as jnp
from jax import lax
from jax.experimental import pallas as pl
from jax.experimental.pallas import tpu as pltpu
from jax.sharding import PartitionSpec as P

EPSILON = 1e-06
MESH = pl.DeviceIdType.MESH
LANES = 128
ROUNDS = 5
SHARES = 3
AT = 64
STEP = 16
NT = (((1,), (1,)), ((), ()))
LOW = jnp.bfloat16
WIDE = jnp.float32


def least_squares(start_norm, columns):
    cosines = []
    sine_terms = []
    triangle = []
    target = [start_norm] + [jnp.zeros_like(start_norm) for j in range(len(columns))]
    for j, column in enumerate(columns):
        column = list(column)
        for i in range(j):
            upper_value = cosines[i] * column[i] + sine_terms[i] * column[i + 1]
            column[i + 1] = -sine_terms[i] * column[i] + cosines[i] * column[i + 1]
            column[i] = upper_value
        radius = jnp.sqrt(column[j] * column[j] + column[j + 1] * column[j + 1])
        cosine = column[j] / radius
        sine_part = column[j + 1] / radius
        column[j] = radius
        target[j + 1] = -sine_part * target[j]
        target[j] = cosine * target[j]
        cosines.append(cosine)
        sine_terms.append(sine_part)
        triangle.append(column[: j + 1])
    weights = [None] * len(columns)
    for j in reversed(range(len(columns))):
        running = target[j]
        for k in range(j + 1, len(columns)):
            running = running - triangle[k][j] * weights[k]
        weights[j] = running / triangle[j][j]
    return weights


def kernel(
    sizes,
    right_ref,
    own_hbm,
    couple_hbm,
    inverse_hbm,
    basis_ref,
    coarse_ref,
    listed_ref,
    picked_ref,
    counts_ref,
    solution_ref,
    next_ref,
    own_ref,
    couple_ref,
    inverse_ref,
    sent,
    held_0,
    held_1,
    held_2,
    held_3,
    held_4,
    share,
    pick,
    coarse_wide,
    basis_parts,
    shifted,
    shifted_parts,
    load_sems,
    send_sem,
    recv_sems,
    share_send_sem,
    share_sems,
):
    subs, crs, cols, rows, kc, slots, share_lanes = sizes
    held = (held_0, held_1, held_2, held_3, held_4)
    me = lax.axis_index("sub")
    mine = lax.axis_index("crs")
    all_rows = float(rows * subs * crs)
    row_of = lax.broadcasted_iota(jnp.int32, (8, LANES), 0)
    lane_of = lax.broadcasted_iota(jnp.int32, (8, LANES), 1)
    top = row_of < 4

    barrier = pltpu.get_barrier_semaphore()

    def greet_sub(i, carry):
        pl.semaphore_signal(
            barrier, inc=1, device_id=(lax.rem(me + i, subs), mine), device_id_type=MESH
        )
        return carry

    def greet_crs(i, carry):
        pl.semaphore_signal(
            barrier, inc=1, device_id=(me, lax.rem(mine + i, crs)), device_id_type=MESH
        )
        return carry

    lax.fori_loop(1, subs, greet_sub, 0)
    lax.fori_loop(1, crs, greet_crs, 0)

    loads = [
        pltpu.make_async_copy(inverse_hbm.at[0, 0], inverse_ref, load_sems.at[0]),
        pltpu.make_async_copy(own_hbm.at[0, 0], own_ref, load_sems.at[1]),
        pltpu.make_async_copy(couple_hbm.at[0, 0], couple_ref, load_sems.at[2]),
    ]
    for load in loads:
        load.start()

    def swap_halves(block):
        return pltpu.roll(block, 4, 0)

    def stack_parts(block):
        width = block.shape[1]
        high = block.astype(LOW).astype(WIDE)
        low = block - high
        at_top = lax.broadcasted_iota(jnp.int32, (8, width), 0) < 4
        return jnp.where(at_top, high, pltpu.roll(low, 4, 0)).astype(LOW)

    def nt(a, b):
        return lax.dot_general(a, b, NT, preferred_element_type=WIDE)

    def nn(a, b):
        return jnp.dot(a, b, preferred_element_type=WIDE)

    def row_sum(a):
        return jnp.sum(a, axis=1, keepdims=True)

    def restrict(block):
        parts = stack_parts(block)
        both = nt(parts, basis_parts[0]) + nt(parts, basis_parts[1])
        return both + swap_halves(both)

    def encode(scalars):
        spread = jnp.zeros((8, LANES), WIDE)
        for d, value in enumerate(scalars):
            spread = jnp.where(lane_of == AT + d, value, spread)
        high = spread.astype(LOW).astype(WIDE)
        rest = spread - high
        middle = rest.astype(LOW).astype(WIDE)
        low = rest - middle
        return high + pltpu.roll(middle, STEP, 1) + pltpu.roll(low, 2 * STEP, 1)

    def pack(block, extra):
        first = jnp.where(top, block[:, :LANES], swap_halves(block[:, LANES : 2 * LANES]))
        second = jnp.where(top, block[:, 2 * LANES :], swap_halves(extra))
        return jnp.concatenate([first, second], axis=0).astype(LOW)

    def send(number, tile):
        sent[number] = tile
        held[number][me] = tile

        def one(i, carry):
            pltpu.make_async_remote_copy(
                src_ref=sent.at[number],
                dst_ref=held[number].at[me],
                send_sem=send_sem,
                recv_sem=recv_sems.at[number],
                device_id=(lax.rem(me + i, subs), mine),
                device_id_type=MESH,
            ).start()
            return carry

        lax.fori_loop(1, subs, one, 0)

    def receive(number):
        arrived = held[number].at[pl.ds(0, subs - 1)]
        pltpu.make_async_copy(arrived, arrived, recv_sems.at[number]).wait()

    def send_share(number, block):
        share[number, mine] = block

        def one(i, carry):
            pltpu.make_async_remote_copy(
                src_ref=share.at[number, mine],
                dst_ref=share.at[number, mine],
                send_sem=share_send_sem,
                recv_sem=share_sems.at[number],
                device_id=(me, lax.rem(mine + i, crs)),
                device_id_type=MESH,
            ).start()
            return carry

        lax.fori_loop(1, crs, one, 0)

    def receive_share(number):
        arrived = share.at[number, pl.ds(0, crs - 1)]
        pltpu.make_async_copy(arrived, arrived, share_sems.at[number]).wait()
        total = share[number, 0]
        for c in range(1, crs):
            total = total + share[number, c]
        return total

    def margin(number):
        lines = []
        for j in range(slots):
            tile = held[number][listed_ref[0, 0, j]].astype(WIDE)
            first = tile[:8]
            lines.append(jnp.concatenate([first, swap_halves(first), tile[8:]], axis=1))
        fetched = nn(jnp.concatenate(lines, axis=0).astype(LOW), pick[...])
        parts = [
            fetched[8 * j : 8 * j + 8, LANES * j : LANES * j + LANES] for j in range(slots)
        ]
        return jnp.concatenate(parts, axis=1).astype(LOW)

    def summed(number):
        total = held[number][0].astype(WIDE)[8:]
        for s in range(1, subs):
            total = total + held[number][s].astype(WIDE)[8:]
        return total + pltpu.roll(total, LANES - STEP, 1) + pltpu.roll(total, LANES - 2 * STEP, 1)

    def coarse_share(number):
        wide = jnp.concatenate([held[number][s] for s in range(subs)], axis=1)
        return nt(wide, coarse_wide[...])[8:]

    def with_scalars(solved, totals):
        if share_lanes > LANES:
            totals = jnp.concatenate(
                [totals, jnp.zeros((8, share_lanes - LANES), WIDE)], axis=1
            )
        at_top = lax.broadcasted_iota(jnp.int32, (8, share_lanes), 0) < 4
        return jnp.where(at_top, pltpu.roll(solved, 4, 0), totals)

    def scalar(block, d):
        return row_sum(jnp.where(lane_of == AT + d, block, 0.0))

    def prolong(total):
        parts = stack_parts(total)
        both = nn(parts, shifted_parts[0]) + nn(parts, shifted_parts[1])
        return both + pltpu.roll(both, 4, 0)

    def precondition(number, share_number, own_part):
        receive(number)
        solved = coarse_share(number)
        totals = summed(number)
        send_share(share_number, with_scalars(solved, totals))
        fine = own_part + nt(margin(number), inverse_ref[:, rows:])
        total = receive_share(share_number)
        return fine + prolong(total), swap_halves(total[:, :LANES])

    right = jnp.concatenate(
        [right_ref[...], jnp.zeros((8 - cols, rows), WIDE)], axis=0
    )
    basis = basis_ref[0, 0]
    basis_full = jnp.concatenate([basis, jnp.zeros((LANES - kc, rows), WIDE)], axis=0)
    basis_high = basis_full.astype(LOW)
    basis_parts[0] = basis_high
    basis_parts[1] = (basis_full - basis_high.astype(WIDE)).astype(LOW)
    extra = restrict(right) + encode([row_sum(right * right)])
    tile = pack(right, extra)
    pl.semaphore_wait(barrier, subs - 1 + crs - 1)
    send(0, tile)

    live = lax.broadcasted_iota(jnp.int32, (slots, LANES), 0) < counts_ref[0, 0]
    wanted = jnp.where(live, picked_ref[0, 0], -1)
    row_index = lax.broadcasted_iota(jnp.int32, (rows, LANES), 0)
    for j in range(slots):
        pick[:, j * LANES : (j + 1) * LANES] = jnp.where(
            row_index == wanted[j : j + 1], 1.0, 0.0
        ).astype(LOW)
    shifted[...] = jnp.zeros_like(shifted)
    shifted[pl.ds(pl.multiple_of(mine * kc, 8), kc), :] = basis
    shifted_full = shifted[...]
    shifted_high = shifted_full.astype(LOW)
    shifted_parts[0] = shifted_high
    shifted_parts[1] = (shifted_full - shifted_high.astype(WIDE)).astype(LOW)
    coarse_rows = crs * kc
    coarse_wide[...] = jnp.zeros_like(coarse_wide)
    coarse_lane = lax.broadcasted_iota(jnp.int32, (coarse_rows, LANES), 1)
    for s in range(subs):
        base = s * kc // LANES * LANES
        offset = s * kc - base
        width = LANES if offset + kc <= LANES else 2 * LANES
        window = coarse_ref[:, base : base + width].astype(WIDE)
        if offset:
            window = pltpu.roll(window, width - offset, 1)
        coarse_wide[:coarse_rows, s * LANES : (s + 1) * LANES] = jnp.where(
            coarse_lane < kc, window[:, :LANES], 0.0
        ).astype(LOW)
    loads[0].wait()
    own_fine = nt(right.astype(LOW), inverse_ref[:, :rows])

    first_z, totals = precondition(0, 0, own_fine)
    right_square = scalar(totals, 0) / all_rows
    start = jnp.sqrt(right_square + EPSILON)

    nothing = jnp.zeros((8, LANES), WIDE)
    send(1, pack(first_z, nothing))
    loads[1].wait()
    loads[2].wait()
    own_part = nt(first_z.astype(LOW), own_ref[...])
    receive(1)
    mapped = own_part + nt(margin(1), couple_ref[...])

    extra = restrict(mapped) + encode([row_sum(mapped * right)])
    send(2, pack(mapped, extra))
    own_fine = nt(mapped.astype(LOW), inverse_ref[:, :rows])
    mapped_z, totals = precondition(2, 1, own_fine)
    height_11 = scalar(totals, 0) / all_rows / (start * start)
    second_z = mapped_z - height_11 * first_z
    second = mapped - height_11 * right

    send(3, pack(second_z, nothing))
    own_part = nt(second_z.astype(LOW), own_ref[...])
    products = [row_sum(second * second), row_sum(right * second)]
    receive(3)
    last = own_part + nt(margin(3), couple_ref[...])

    products = products + [row_sum(last * right), row_sum(last * second), row_sum(last * last)]
    send(4, pack(jnp.zeros((8, rows), WIDE), encode(products)))
    receive(4)
    totals = summed(4)
    send_share(2, with_scalars(jnp.zeros((8, share_lanes), WIDE), totals))
    totals = swap_halves(receive_share(2)[:, :LANES])
    second_square = scalar(totals, 0) / all_rows
    length_1 = jnp.sqrt(second_square / (start * start) + EPSILON)
    scale = 1.0 / (start * length_1)
    start_scale = 1.0 / start
    gram_11 = right_square * start_scale * start_scale
    gram_12 = scalar(totals, 1) / all_rows * start_scale * scale
    gram_22 = second_square * scale * scale
    height_12 = scalar(totals, 2) / all_rows * start_scale * scale
    height_22 = scalar(totals, 3) / all_rows * scale * scale
    last_square = scalar(totals, 4) / all_rows * scale * scale
    rest = (
        last_square
        - height_12 * height_12 * (2.0 - gram_11)
        - height_22 * height_22 * (2.0 - gram_22)
        + 2.0 * height_12 * height_22 * gram_12
    )
    length_2 = jnp.sqrt(jnp.maximum(rest, 0.0) + EPSILON)
    weights = least_squares(start, [[height_11, length_1], [height_12, height_22, length_2]])
    result = (weights[0] * start_scale) * first_z + (weights[1] * scale) * second_z
    following = (last * scale - (height_12 * start_scale) * right - (height_22 * scale) * second) / length_2
    solution_ref[...] = result[:cols]
    next_ref[...] = following[:cols]

    def drain(i, carry):
        pltpu.make_async_copy(sent.at[0], sent.at[0], send_sem).wait()
        return carry

    lax.fori_loop(0, ROUNDS * (subs - 1), drain, 0)

    def drain_share(i, carry):
        pltpu.make_async_copy(share.at[0, 0], share.at[0, 0], share_send_sem).wait()
        return carry

    lax.fori_loop(0, SHARES * (crs - 1), drain_share, 0)


def body(
    right_side,
    own_block,
    coupling,
    local_inverse,
    coarse_basis,
    coarse_inverse,
    neighbours,
    margin_rows,
    block_counts,
):
    cols, rows = right_side.shape[0], right_side.shape[3]
    subs, crs = lax.axis_size("sub"), lax.axis_size("crs")
    kc = coarse_basis.shape[2]
    slots, block_rows = margin_rows.shape[2:]
    coarse_rows = crs * kc
    share_lanes = -(-coarse_rows // LANES) * LANES
    sizes = (subs, crs, cols, rows, kc, slots, share_lanes)
    vmem = pl.BlockSpec(memory_space=pltpu.VMEM)
    smem = pl.BlockSpec(memory_space=pltpu.SMEM)
    anywhere = pl.BlockSpec(memory_space=pl.ANY)
    out = jax.ShapeDtypeStruct((cols, rows), WIDE)
    result, following = pl.pallas_call(
        functools.partial(kernel, sizes),
        out_shape=(out, out),
        in_specs=[vmem, anywhere, anywhere, anywhere, vmem, vmem, smem, vmem, smem],
        out_specs=(vmem, vmem),
        scratch_shapes=[
            pltpu.VMEM((rows, rows), LOW),
            pltpu.VMEM((rows, slots * block_rows), LOW),
            pltpu.VMEM((rows, rows + slots * block_rows), LOW),
            pltpu.VMEM((ROUNDS, 16, LANES), LOW),
            *[pltpu.VMEM((subs, 16, LANES), LOW) for number in range(ROUNDS)],
            pltpu.VMEM((SHARES, crs, 8, share_lanes), WIDE),
            pltpu.VMEM((rows, slots * block_rows), LOW),
            pltpu.VMEM((share_lanes, subs * LANES), LOW),
            pltpu.VMEM((2, LANES, rows), LOW),
            pltpu.VMEM((share_lanes, rows), WIDE),
            pltpu.VMEM((2, share_lanes, rows), LOW),
            pltpu.SemaphoreType.DMA((3,)),
            pltpu.SemaphoreType.DMA,
            pltpu.SemaphoreType.DMA((ROUNDS,)),
            pltpu.SemaphoreType.DMA,
            pltpu.SemaphoreType.DMA((SHARES,)),
        ],
        compiler_params=pltpu.CompilerParams(
            collective_id=0, has_side_effects=True, vmem_limit_bytes=40 * 1024 * 1024
        ),
    )(
        right_side.reshape(cols, rows),
        own_block,
        coupling,
        local_inverse,
        coarse_basis,
        coarse_inverse.reshape(coarse_rows, -1),
        neighbours,
        margin_rows,
        block_counts,
    )
    shape = (cols, 1, 1, rows)
    return result.reshape(shape), following.reshape(shape)


def solution(mesh):
    in_specs = (
        P(None, "sub", "crs", None),
        P("sub", "crs", None, None),
        P("sub", "crs", None, None),
        P("sub", "crs", None, None),
        P("sub", "crs", None, None),
        P("sub", None, "crs", None),
        P("sub", "crs", None),
        P("sub", "crs", None, None),
        P("sub", "crs"),
    )
    out_specs = (P(None, "sub", "crs", None), P(None, "sub", "crs", None))
    return jax.shard_map(body, mesh=mesh, in_specs=in_specs, out_specs=out_specs, check_vma=False)
```

```python
import functools

import jax
import jax.numpy as jnp
from jax import lax
from jax.experimental import pallas as pl
from jax.experimental.pallas import tpu as pltpu
from jax.sharding import PartitionSpec as P

EPSILON = 1e-06
MESH = pl.DeviceIdType.MESH
LANES = 128
ROUNDS = 4
SHARES = 2
AT = 120
NT = (((1,), (1,)), ((), ()))
LOW = jnp.bfloat16
WIDE = jnp.float32


def least_squares(start_norm, columns):
    cosines = []
    sine_terms = []
    triangle = []
    target = [start_norm] + [jnp.zeros_like(start_norm) for j in range(len(columns))]
    for j, column in enumerate(columns):
        column = list(column)
        for i in range(j):
            upper_value = cosines[i] * column[i] + sine_terms[i] * column[i + 1]
            column[i + 1] = -sine_terms[i] * column[i] + cosines[i] * column[i + 1]
            column[i] = upper_value
        radius = jnp.sqrt(column[j] * column[j] + column[j + 1] * column[j + 1])
        cosine = column[j] / radius
        sine_part = column[j + 1] / radius
        column[j] = radius
        target[j + 1] = -sine_part * target[j]
        target[j] = cosine * target[j]
        cosines.append(cosine)
        sine_terms.append(sine_part)
        triangle.append(column[: j + 1])
    weights = [None] * len(columns)
    for j in reversed(range(len(columns))):
        running = target[j]
        for k in range(j + 1, len(columns)):
            running = running - triangle[k][j] * weights[k]
        weights[j] = running / triangle[j][j]
    return weights


def kernel(
    sizes,
    right_hbm,
    own_hbm,
    couple_hbm,
    inverse_hbm,
    basis_hbm,
    coarse_hbm,
    listed_hbm,
    picked_hbm,
    counts_hbm,
    both_ref,
    right_ref,
    own_ref,
    couple_ref,
    inverse_ref,
    basis_ref,
    coarse_ref,
    listed_ref,
    picked_ref,
    counts_ref,
    sent,
    held_0,
    held_1,
    held_2,
    held_3,
    share,
    last_rows,
    pick,
    coarse_wide,
    placed,
    basis_parts,
    shifted,
    shifted_parts,
    load_sems,
    send_sem,
    recv_sems,
    share_send_sem,
    share_sems,
    last_send_sem,
    last_sem,
):
    subs, crs, cols, rows, kc, slots, share_lanes, together, groups = sizes
    held = (held_0, held_1, held_2, held_3)
    me = lax.axis_index("sub")
    mine = lax.axis_index("crs")
    all_rows = float(rows * subs * crs)
    row_of = lax.broadcasted_iota(jnp.int32, (8, LANES), 0)
    lane_of = lax.broadcasted_iota(jnp.int32, (8, LANES), 1)
    top = row_of < 4

    pairs = [
        (right_hbm, right_ref),
        (basis_hbm, basis_ref),
        (picked_hbm, picked_ref),
        (counts_hbm, counts_ref),
        (coarse_hbm, coarse_ref),
        (listed_hbm, listed_ref),
        (inverse_hbm, inverse_ref),
        (own_hbm, own_ref),
        (couple_hbm, couple_ref),
    ]
    loads = [
        pltpu.make_async_copy(there, here, load_sems.at[n])
        for n, (there, here) in enumerate(pairs)
    ]
    for load in loads:
        load.start()
    barrier = pltpu.get_barrier_semaphore()

    def greet_sub(i, carry):
        pl.semaphore_signal(
            barrier, inc=1, device_id=(lax.rem(me + i, subs), mine), device_id_type=MESH
        )
        return carry

    def greet_crs(i, carry):
        pl.semaphore_signal(
            barrier, inc=1, device_id=(me, lax.rem(mine + i, crs)), device_id_type=MESH
        )
        return carry

    lax.fori_loop(1, subs, greet_sub, 0)
    lax.fori_loop(1, crs, greet_crs, 0)


    def swap_halves(block):
        return pltpu.roll(block, 4, 0)

    def stack_parts(block):
        width = block.shape[1]
        high = block.astype(LOW).astype(WIDE)
        low = block - high
        at_top = lax.broadcasted_iota(jnp.int32, (8, width), 0) < 4
        return jnp.where(at_top, high, pltpu.roll(low, 4, 0)).astype(LOW)

    def nt(a, b):
        return lax.dot_general(a, b, NT, preferred_element_type=WIDE)

    def nn(a, b):
        return jnp.dot(a, b, preferred_element_type=WIDE)

    def row_sum(a):
        return jnp.sum(a, axis=1, keepdims=True)

    def restrict(block):
        parts = stack_parts(block)
        both = nt(parts, basis_parts[0]) + nt(parts, basis_parts[1])
        return both + swap_halves(both)

    def encode(value):
        high = value.astype(LOW).astype(WIDE)
        rest = value - high
        middle = rest.astype(LOW).astype(WIDE)
        low = rest - middle
        spread = jnp.where(lane_of == AT, high, 0.0)
        spread = jnp.where(lane_of == AT + 1, middle, spread)
        return jnp.where(lane_of == AT + 2, low, spread)

    def pack(block, extra):
        first = jnp.where(top, block[:, :LANES], swap_halves(block[:, LANES : 2 * LANES]))
        second = jnp.where(top, block[:, 2 * LANES :], swap_halves(extra))
        return jnp.concatenate([first, second], axis=0).astype(LOW)

    def send(number, tile):
        sent[number] = tile

        def one(i, carry):
            pltpu.make_async_remote_copy(
                src_ref=sent.at[number],
                dst_ref=held[number].at[me],
                send_sem=send_sem,
                recv_sem=recv_sems.at[number],
                device_id=(lax.rem(me + i, subs), mine),
                device_id_type=MESH,
            ).start()
            return carry

        lax.fori_loop(1, subs, one, 0)

    def receive(number):
        arrived = held[number].at[pl.ds(0, subs - 1)]
        pltpu.make_async_copy(arrived, arrived, recv_sems.at[number]).wait()

    def send_share(number, block):
        share[number, mine] = block

        def one(i, carry):
            pltpu.make_async_remote_copy(
                src_ref=share.at[number, mine],
                dst_ref=share.at[number, mine],
                send_sem=share_send_sem,
                recv_sem=share_sems.at[number],
                device_id=(me, lax.rem(mine + i, crs)),
                device_id_type=MESH,
            ).start()
            return carry

        lax.fori_loop(1, crs, one, 0)

    def receive_share(number):
        arrived = share.at[number, pl.ds(0, crs - 1)]
        pltpu.make_async_copy(arrived, arrived, share_sems.at[number]).wait()
        total = share[number, 0]
        for c in range(1, crs):
            total = total + share[number, c]
        return total

    def margin(number):
        lines = []
        for j in range(slots):
            tile = held[number][listed_ref[0, 0, j]].astype(WIDE)
            first = tile[:8]
            lines.append(jnp.concatenate([first, swap_halves(first), tile[8:]], axis=1))
        fetched = nn(jnp.concatenate(lines, axis=0).astype(LOW), pick[...])
        parts = [
            fetched[8 * j : 8 * j + 8, LANES * j : LANES * j + LANES] for j in range(slots)
        ]
        return jnp.concatenate(parts, axis=1).astype(LOW)

    def group_sums(number):
        sums = []
        for g in range(groups):
            members = range(g * together, min(subs, (g + 1) * together))
            tiles = [held[number][s].astype(WIDE)[8:] for s in members]
            sums.append(functools.reduce(jnp.add, tiles))
        return sums

    def with_scalars(solved, totals):
        if share_lanes > LANES:
            totals = jnp.concatenate(
                [totals, jnp.zeros((8, share_lanes - LANES), WIDE)], axis=1
            )
        at_top = lax.broadcasted_iota(jnp.int32, (8, share_lanes), 0) < 4
        return jnp.where(at_top, pltpu.roll(solved, 4, 0), totals)

    def scalar(block):
        return row_sum(jnp.where((lane_of >= AT) & (lane_of < AT + 3), block, 0.0))

    def prolong(total):
        parts = stack_parts(total)
        both = nn(parts, shifted_parts[0]) + nn(parts, shifted_parts[1])
        return both + pltpu.roll(both, 4, 0)

    def precondition(number, share_number, own_part):
        receive(number)
        sums = group_sums(number)
        solved = nt(jnp.concatenate(sums, axis=1).astype(LOW), coarse_wide[...])
        totals = functools.reduce(jnp.add, sums)
        send_share(share_number, with_scalars(solved, totals))
        fine = own_part + nt(margin(number), inverse_ref[:, rows:])
        total = receive_share(share_number)
        return fine + prolong(total), swap_halves(total[:, :LANES])

    loads[0].wait()
    loads[1].wait()
    right = jnp.concatenate(
        [right_ref[q] for q in range(cols)] + [jnp.zeros((8 - cols, rows), WIDE)], axis=0
    )
    basis = basis_ref[0, 0]
    placed[...] = jnp.zeros_like(placed)
    placed[pl.ds(pl.multiple_of(lax.rem(me, together) * kc, 8), kc), :] = basis
    basis_full = placed[...]
    basis_high = basis_full.astype(LOW)
    basis_parts[0] = basis_high
    basis_parts[1] = (basis_full - basis_high.astype(WIDE)).astype(LOW)
    extra = restrict(right) + encode(row_sum(right * right))
    tile = pack(right, extra)
    held_0[me] = tile
    pl.semaphore_wait(barrier, subs - 1 + crs - 1)
    send(0, tile)

    loads[2].wait()
    loads[3].wait()
    live = lax.broadcasted_iota(jnp.int32, (slots, LANES), 0) < counts_ref[0, 0]
    wanted = jnp.where(
        live, jnp.concatenate([picked_ref[0, j] for j in range(slots)], axis=0), -1
    )
    row_index = lax.broadcasted_iota(jnp.int32, (rows, LANES), 0)
    for j in range(slots):
        pick[:, j * LANES : (j + 1) * LANES] = jnp.where(
            row_index == wanted[j : j + 1], 1.0, 0.0
        ).astype(LOW)
    shifted[...] = jnp.zeros_like(shifted)
    shifted[pl.ds(pl.multiple_of(mine * kc, 8), kc), :] = basis
    shifted_full = shifted[...]
    shifted_high = shifted_full.astype(LOW)
    shifted_parts[0] = shifted_high
    shifted_parts[1] = (shifted_full - shifted_high.astype(WIDE)).astype(LOW)
    loads[4].wait()
    coarse_rows = crs * kc
    coarse_cols = subs * kc
    coarse_wide[...] = jnp.zeros_like(coarse_wide)
    coarse_lane = lax.broadcasted_iota(jnp.int32, (coarse_rows, LANES), 1)
    for g in range(groups):
        first = g * together * kc
        count = min(together * kc, coarse_cols - first)
        base = first // LANES * LANES
        offset = first - base
        width = LANES if offset + count <= LANES else 2 * LANES
        window = coarse_ref[:, base : base + width].astype(WIDE)
        if offset:
            window = pltpu.roll(window, width - offset, 1)
        coarse_wide[:coarse_rows, g * LANES : (g + 1) * LANES] = jnp.where(
            coarse_lane < count, window[:, :LANES], 0.0
        ).astype(LOW)
    loads[5].wait()
    loads[6].wait()
    own_fine = nt(right.astype(LOW), inverse_ref[:, :rows])

    first_z, totals = precondition(0, 0, own_fine)
    right_square = scalar(totals) / all_rows
    start = jnp.sqrt(right_square + EPSILON)

    nothing = jnp.zeros((8, LANES), WIDE)
    send(1, pack(first_z, nothing))
    loads[7].wait()
    loads[8].wait()
    own_part = nt(first_z.astype(LOW), own_ref[...])
    receive(1)
    mapped = own_part + nt(margin(1), couple_ref[...])

    extra = restrict(mapped) + encode(row_sum(mapped * right))
    tile = pack(mapped, extra)
    held_2[me] = tile
    send(2, tile)
    own_fine = nt(mapped.astype(LOW), inverse_ref[:, :rows])
    mapped_z, totals = precondition(2, 1, own_fine)
    height_11 = scalar(totals) / all_rows / (start * start)
    second_z = mapped_z - height_11 * first_z
    second = mapped - height_11 * right

    send(3, pack(second_z, nothing))
    own_part = nt(second_z.astype(LOW), own_ref[...])
    products = [row_sum(second * second), row_sum(right * second)]
    receive(3)
    last = own_part + nt(margin(3), couple_ref[...])

    products = products + [row_sum(last * right), row_sum(last * second), row_sum(last * last)]
    line = jnp.zeros((8, LANES), WIDE)
    for d, value in enumerate(products):
        line = jnp.where((lane_of == d * 4 + row_of) & top, value, line)
    here = me * crs + mine
    everyone = subs * crs
    last_rows[here] = jnp.sum(line, axis=0, keepdims=True)

    def send_last(i, carry):
        there = lax.rem(here + i, everyone)
        pltpu.make_async_remote_copy(
            src_ref=last_rows.at[here],
            dst_ref=last_rows.at[here],
            send_sem=last_send_sem,
            recv_sem=last_sem,
            device_id=(there // crs, lax.rem(there, crs)),
            device_id_type=MESH,
        ).start()
        return carry

    lax.fori_loop(1, everyone, send_last, 0)
    arrived = last_rows.at[pl.ds(0, everyone - 1)]
    pltpu.make_async_copy(arrived, arrived, last_sem).wait()
    whole = jnp.broadcast_to(jnp.sum(last_rows[...], axis=0), (8, LANES)) / all_rows

    def final(d):
        return row_sum(jnp.where(lane_of == d * 4 + row_of, whole, 0.0))

    second_square = final(0)
    length_1 = jnp.sqrt(second_square / (start * start) + EPSILON)
    scale = 1.0 / (start * length_1)
    start_scale = 1.0 / start
    gram_11 = right_square * start_scale * start_scale
    gram_12 = final(1) * start_scale * scale
    gram_22 = second_square * scale * scale
    height_12 = final(2) * start_scale * scale
    height_22 = final(3) * scale * scale
    last_square = final(4) * scale * scale
    rest = (
        last_square
        - height_12 * height_12 * (2.0 - gram_11)
        - height_22 * height_22 * (2.0 - gram_22)
        + 2.0 * height_12 * height_22 * gram_12
    )
    length_2 = jnp.sqrt(jnp.maximum(rest, 0.0) + EPSILON)
    weights = least_squares(start, [[height_11, length_1], [height_12, height_22, length_2]])
    result = (weights[0] * start_scale) * first_z + (weights[1] * scale) * second_z
    following = (last * scale - (height_12 * start_scale) * right - (height_22 * scale) * second) / length_2
    for q in range(cols):
        both_ref[0, q] = result[q : q + 1]
        both_ref[1, q] = following[q : q + 1]

    for number in range(ROUNDS):
        gone = held[number].at[pl.ds(0, subs - 1)]
        pltpu.make_async_copy(gone, gone, send_sem).wait()
    for number in range(SHARES):
        gone = share.at[number, pl.ds(0, crs - 1)]
        pltpu.make_async_copy(gone, gone, share_send_sem).wait()
    pltpu.make_async_copy(arrived, arrived, last_send_sem).wait()


def body(
    right_side,
    own_block,
    coupling,
    local_inverse,
    coarse_basis,
    coarse_inverse,
    neighbours,
    margin_rows,
    block_counts,
):
    cols, rows = right_side.shape[0], right_side.shape[3]
    subs, crs = lax.axis_size("sub"), lax.axis_size("crs")
    kc = coarse_basis.shape[2]
    slots, block_rows = margin_rows.shape[2:]
    coarse_rows = crs * kc
    share_lanes = -(-coarse_rows // LANES) * LANES
    together = (LANES - 8) // kc
    groups = -(-subs // together)
    sizes = (subs, crs, cols, rows, kc, slots, share_lanes, together, groups)
    vmem = pl.BlockSpec(memory_space=pltpu.VMEM)
    stays = pl.BlockSpec(memory_space=pltpu.HBM)
    both = pl.pallas_call(
        functools.partial(kernel, sizes),
        out_shape=jax.ShapeDtypeStruct((2, cols, 1, rows), WIDE),
        in_specs=[stays] * 9,
        out_specs=vmem,
        scratch_shapes=[
            pltpu.VMEM((cols, 1, rows), WIDE),
            pltpu.VMEM((rows, rows), LOW),
            pltpu.VMEM((rows, slots * block_rows), LOW),
            pltpu.VMEM((rows, rows + slots * block_rows), LOW),
            pltpu.VMEM((1, 1, kc, rows), WIDE),
            pltpu.VMEM((coarse_rows, subs * kc), LOW),
            pltpu.SMEM((1, 1, slots), jnp.int32),
            pltpu.VMEM((1, slots, 1, block_rows), jnp.int32),
            pltpu.SMEM((1, 1), jnp.int32),
            pltpu.VMEM((ROUNDS, 16, LANES), LOW),
            *[pltpu.VMEM((subs, 16, LANES), LOW) for number in range(ROUNDS)],
            pltpu.VMEM((SHARES, crs, 8, share_lanes), WIDE),
            pltpu.VMEM((subs * crs, 1, LANES), WIDE),
            pltpu.VMEM((rows, slots * block_rows), LOW),
            pltpu.VMEM((share_lanes, groups * LANES), LOW),
            pltpu.VMEM((LANES, rows), WIDE),
            pltpu.VMEM((2, LANES, rows), LOW),
            pltpu.VMEM((share_lanes, rows), WIDE),
            pltpu.VMEM((2, share_lanes, rows), LOW),
            pltpu.SemaphoreType.DMA((9,)),
            pltpu.SemaphoreType.DMA,
            pltpu.SemaphoreType.DMA((ROUNDS,)),
            pltpu.SemaphoreType.DMA,
            pltpu.SemaphoreType.DMA((SHARES,)),
            pltpu.SemaphoreType.DMA,
            pltpu.SemaphoreType.DMA,
        ],
        compiler_params=pltpu.CompilerParams(
            collective_id=0, has_side_effects=True, vmem_limit_bytes=63 * 1024 * 1024
        ),
    )(
        right_side.reshape(cols, 1, rows),
        own_block.reshape(rows, -1),
        coupling.reshape(rows, -1),
        local_inverse.reshape(rows, -1),
        coarse_basis,
        coarse_inverse.reshape(coarse_rows, -1),
        neighbours,
        margin_rows.reshape(1, slots, 1, block_rows),
        block_counts,
    )
    shape = (cols, 1, 1, rows)
    return both[0].reshape(shape), both[1].reshape(shape)


def solution(mesh):
    in_specs = (
        P(None, "sub", "crs", None),
        P("sub", "crs", None, None),
        P("sub", "crs", None, None),
        P("sub", "crs", None, None),
        P("sub", "crs", None, None),
        P("sub", None, "crs", None),
        P("sub", "crs", None),
        P("sub", "crs", None, None),
        P("sub", "crs"),
    )
    out_specs = (P(None, "sub", "crs", None), P(None, "sub", "crs", None))
    return jax.shard_map(body, mesh=mesh, in_specs=in_specs, out_specs=out_specs, check_vma=False)
```

```python
import functools

import jax
import jax.numpy as jnp
from jax import lax
from jax.experimental import pallas as pl
from jax.experimental.pallas import tpu as pltpu
from jax.sharding import PartitionSpec as P

EPSILON = 1e-06
MESH = pl.DeviceIdType.MESH
LANES = 128
ROUNDS = 4
SHARES = 2
ORDER = (15, 11, 14, 13, 10, 9, 12, 8, 7, 6, 5, 4, 3, 2, 1)
AT = 120
NT = (((1,), (1,)), ((), ()))
LOW = jnp.bfloat16
WIDE = jnp.float32


def least_squares(start_norm, columns):
    cosines = []
    sine_terms = []
    triangle = []
    target = [start_norm] + [jnp.zeros_like(start_norm) for j in range(len(columns))]
    for j, column in enumerate(columns):
        column = list(column)
        for i in range(j):
            upper_value = cosines[i] * column[i] + sine_terms[i] * column[i + 1]
            column[i + 1] = -sine_terms[i] * column[i] + cosines[i] * column[i + 1]
            column[i] = upper_value
        radius = jnp.sqrt(column[j] * column[j] + column[j + 1] * column[j + 1])
        cosine = column[j] / radius
        sine_part = column[j + 1] / radius
        column[j] = radius
        target[j + 1] = -sine_part * target[j]
        target[j] = cosine * target[j]
        cosines.append(cosine)
        sine_terms.append(sine_part)
        triangle.append(column[: j + 1])
    weights = [None] * len(columns)
    for j in reversed(range(len(columns))):
        running = target[j]
        for k in range(j + 1, len(columns)):
            running = running - triangle[k][j] * weights[k]
        weights[j] = running / triangle[j][j]
    return weights


def kernel(
    sizes,
    right_hbm,
    own_hbm,
    couple_hbm,
    inverse_hbm,
    basis_hbm,
    coarse_hbm,
    listed_hbm,
    picked_hbm,
    counts_hbm,
    both_ref,
    right_ref,
    own_ref,
    couple_ref,
    inverse_ref,
    basis_ref,
    coarse_ref,
    listed_ref,
    picked_ref,
    counts_ref,
    sent,
    held_0,
    held_1,
    held_2,
    held_3,
    share,
    last_rows,
    pick,
    coarse_wide,
    placed,
    basis_parts,
    shifted,
    shifted_parts,
    load_sems,
    send_sem,
    recv_sems,
    share_send_sem,
    share_sems,
    last_send_sem,
    last_sem,
):
    subs, crs, cols, rows, kc, slots, share_lanes, together, groups = sizes
    held = (held_0, held_1, held_2, held_3)
    me = lax.axis_index("sub")
    mine = lax.axis_index("crs")
    all_rows = float(rows * subs * crs)
    row_of = lax.broadcasted_iota(jnp.int32, (8, LANES), 0)
    lane_of = lax.broadcasted_iota(jnp.int32, (8, LANES), 1)
    top = row_of < 4

    barrier = pltpu.get_barrier_semaphore()

    short = subs & (subs - 1) == 0 and subs <= 16

    def flipped(index, mask, bits):
        moved = index
        for k in range(bits):
            if mask >> k & 1:
                moved = moved + (1 << k) - (index // (1 << k)) % 2 * (2 << k)
        return moved

    def each_sub(act):
        if short:
            for mask in ORDER:
                if mask < subs:
                    act(flipped(me, mask, 4))
        else:

            def one(i, carry):
                act(lax.rem(me + i, subs))
                return carry

            lax.fori_loop(1, subs, one, 0)

    def each_crs(act):
        def one(i, carry):
            act(lax.rem(mine + i, crs))
            return carry

        if crs == 2:
            act(1 - mine)
        else:
            lax.fori_loop(1, crs, one, 0)

    def greet(sub, core):
        pl.semaphore_signal(barrier, inc=1, device_id=(sub, core), device_id_type=MESH)

    each_sub(lambda sub: greet(sub, mine))
    each_crs(lambda core: greet(me, core))

    pairs = [
        (right_hbm, right_ref),
        (basis_hbm, basis_ref),
        (picked_hbm, picked_ref),
        (counts_hbm, counts_ref),
        (coarse_hbm, coarse_ref),
        (listed_hbm, listed_ref),
        (inverse_hbm, inverse_ref),
        (own_hbm, own_ref),
        (couple_hbm, couple_ref),
    ]
    loads = [
        pltpu.make_async_copy(there, here, load_sems.at[n])
        for n, (there, here) in enumerate(pairs)
    ]
    for load in loads:
        load.start()

    def swap_halves(block):
        return pltpu.roll(block, 4, 0)

    def stack_parts(block):
        width = block.shape[1]
        high = block.astype(LOW).astype(WIDE)
        low = block - high
        at_top = lax.broadcasted_iota(jnp.int32, (8, width), 0) < 4
        return jnp.where(at_top, high, pltpu.roll(low, 4, 0)).astype(LOW)

    def nt(a, b):
        return lax.dot_general(a, b, NT, preferred_element_type=WIDE)

    def nn(a, b):
        return jnp.dot(a, b, preferred_element_type=WIDE)

    def row_sum(a):
        return jnp.sum(a, axis=1, keepdims=True)

    def restrict(block):
        parts = stack_parts(block)
        both = nt(parts, basis_parts[0]) + nt(parts, basis_parts[1])
        return both + swap_halves(both)

    def encode(value):
        high = value.astype(LOW).astype(WIDE)
        rest = value - high
        middle = rest.astype(LOW).astype(WIDE)
        low = rest - middle
        spread = jnp.where(lane_of == AT, high, 0.0)
        spread = jnp.where(lane_of == AT + 1, middle, spread)
        return jnp.where(lane_of == AT + 2, low, spread)

    def pack(block, extra):
        first = jnp.where(top, block[:, :LANES], swap_halves(block[:, LANES : 2 * LANES]))
        second = jnp.where(top, block[:, 2 * LANES :], swap_halves(extra))
        return jnp.concatenate([first, second], axis=0).astype(LOW)

    def send(number, tile):
        sent[number] = tile

        def one(sub):
            pltpu.make_async_remote_copy(
                src_ref=sent.at[number],
                dst_ref=held[number].at[me],
                send_sem=send_sem,
                recv_sem=recv_sems.at[number],
                device_id=(sub, mine),
                device_id_type=MESH,
            ).start()

        each_sub(one)

    def receive(number):
        arrived = held[number].at[pl.ds(0, subs - 1)]
        pltpu.make_async_copy(arrived, arrived, recv_sems.at[number]).wait()

    def send_share(number, block):
        share[number, mine] = block

        def one(core):
            pltpu.make_async_remote_copy(
                src_ref=share.at[number, mine],
                dst_ref=share.at[number, mine],
                send_sem=share_send_sem,
                recv_sem=share_sems.at[number],
                device_id=(me, core),
                device_id_type=MESH,
            ).start()

        each_crs(one)

    def receive_share(number):
        arrived = share.at[number, pl.ds(0, crs - 1)]
        pltpu.make_async_copy(arrived, arrived, share_sems.at[number]).wait()
        total = share[number, 0]
        for c in range(1, crs):
            total = total + share[number, c]
        return total

    def margin(number):
        lines = []
        for j in range(slots):
            tile = held[number][listed_ref[0, 0, j]].astype(WIDE)
            first = tile[:8]
            lines.append(jnp.concatenate([first, swap_halves(first), tile[8:]], axis=1))
        fetched = nn(jnp.concatenate(lines, axis=0).astype(LOW), pick[...])
        parts = [
            fetched[8 * j : 8 * j + 8, LANES * j : LANES * j + LANES] for j in range(slots)
        ]
        return jnp.concatenate(parts, axis=1).astype(LOW)

    def group_sums(number):
        sums = []
        for g in range(groups):
            members = range(g * together, min(subs, (g + 1) * together))
            tiles = [held[number][s].astype(WIDE)[8:] for s in members]
            sums.append(functools.reduce(jnp.add, tiles))
        return sums

    def with_scalars(solved, totals):
        if share_lanes > LANES:
            totals = jnp.concatenate(
                [totals, jnp.zeros((8, share_lanes - LANES), WIDE)], axis=1
            )
        at_top = lax.broadcasted_iota(jnp.int32, (8, share_lanes), 0) < 4
        return jnp.where(at_top, pltpu.roll(solved, 4, 0), totals)

    def scalar(block):
        return row_sum(jnp.where((lane_of >= AT) & (lane_of < AT + 3), block, 0.0))

    def prolong(total):
        parts = stack_parts(total)
        both = nn(parts, shifted_parts[0]) + nn(parts, shifted_parts[1])
        return both + pltpu.roll(both, 4, 0)

    def precondition(number, share_number, own_part):
        receive(number)
        sums = group_sums(number)
        solved = nt(jnp.concatenate(sums, axis=1).astype(LOW), coarse_wide[...])
        totals = functools.reduce(jnp.add, sums)
        send_share(share_number, with_scalars(solved, totals))
        fine = own_part + nt(margin(number), inverse_ref[:, rows:])
        total = receive_share(share_number)
        return fine + prolong(total), swap_halves(total[:, :LANES])

    loads[0].wait()
    loads[1].wait()
    right = jnp.concatenate(
        [right_ref[q] for q in range(cols)] + [jnp.zeros((8 - cols, rows), WIDE)], axis=0
    )
    basis = basis_ref[0, 0]
    placed[...] = jnp.zeros_like(placed)
    placed[pl.ds(pl.multiple_of(lax.rem(me, together) * kc, 8), kc), :] = basis
    basis_full = placed[...]
    basis_high = basis_full.astype(LOW)
    basis_parts[0] = basis_high
    basis_parts[1] = (basis_full - basis_high.astype(WIDE)).astype(LOW)
    extra = restrict(right) + encode(row_sum(right * right))
    tile = pack(right, extra)
    held_0[me] = tile
    pl.semaphore_wait(barrier, subs - 1 + crs - 1)
    send(0, tile)

    loads[2].wait()
    loads[3].wait()
    live = lax.broadcasted_iota(jnp.int32, (slots, LANES), 0) < counts_ref[0, 0, 0]
    wanted = jnp.where(
        live, jnp.concatenate([picked_ref[0, j] for j in range(slots)], axis=0), -1
    )
    row_index = lax.broadcasted_iota(jnp.int32, (rows, LANES), 0)
    for j in range(slots):
        pick[:, j * LANES : (j + 1) * LANES] = jnp.where(
            row_index == wanted[j : j + 1], 1.0, 0.0
        ).astype(LOW)
    shifted[...] = jnp.zeros_like(shifted)
    shifted[pl.ds(pl.multiple_of(mine * kc, 8), kc), :] = basis
    shifted_full = shifted[...]
    shifted_high = shifted_full.astype(LOW)
    shifted_parts[0] = shifted_high
    shifted_parts[1] = (shifted_full - shifted_high.astype(WIDE)).astype(LOW)
    loads[4].wait()
    coarse_rows = crs * kc
    coarse_cols = subs * kc
    coarse_wide[...] = jnp.zeros_like(coarse_wide)
    coarse_lane = lax.broadcasted_iota(jnp.int32, (coarse_rows, LANES), 1)
    for g in range(groups):
        first = g * together * kc
        count = min(together * kc, coarse_cols - first)
        base = first // LANES * LANES
        offset = first - base
        width = LANES if offset + count <= LANES else 2 * LANES
        window = coarse_ref[:, base : base + width].astype(WIDE)
        if offset:
            window = pltpu.roll(window, width - offset, 1)
        coarse_wide[:coarse_rows, g * LANES : (g + 1) * LANES] = jnp.where(
            coarse_lane < count, window[:, :LANES], 0.0
        ).astype(LOW)
    loads[5].wait()
    loads[6].wait()
    own_fine = nt(right.astype(LOW), inverse_ref[:, :rows])

    first_z, totals = precondition(0, 0, own_fine)
    right_square = scalar(totals) / all_rows
    start = jnp.sqrt(right_square + EPSILON)

    nothing = jnp.zeros((8, LANES), WIDE)
    send(1, pack(first_z, nothing))
    loads[7].wait()
    loads[8].wait()
    own_part = nt(first_z.astype(LOW), own_ref[...])
    receive(1)
    mapped = own_part + nt(margin(1), couple_ref[...])

    extra = restrict(mapped) + encode(row_sum(mapped * right))
    tile = pack(mapped, extra)
    held_2[me] = tile
    send(2, tile)
    own_fine = nt(mapped.astype(LOW), inverse_ref[:, :rows])
    mapped_z, totals = precondition(2, 1, own_fine)
    height_11 = scalar(totals) / all_rows / (start * start)
    second_z = mapped_z - height_11 * first_z
    second = mapped - height_11 * right

    send(3, pack(second_z, nothing))
    own_part = nt(second_z.astype(LOW), own_ref[...])
    products = [row_sum(second * second), row_sum(right * second)]
    receive(3)
    last = own_part + nt(margin(3), couple_ref[...])

    products = products + [row_sum(last * right), row_sum(last * second), row_sum(last * last)]
    line = jnp.zeros((8, LANES), WIDE)
    for d, value in enumerate(products):
        line = jnp.where((lane_of == d * 4 + row_of) & top, value, line)
    here = me * crs + mine
    everyone = subs * crs
    last_rows[here] = jnp.sum(line, axis=0, keepdims=True)

    def send_last(sub, core):
        pltpu.make_async_remote_copy(
            src_ref=last_rows.at[here],
            dst_ref=last_rows.at[here],
            send_sem=last_send_sem,
            recv_sem=last_sem,
            device_id=(sub, core),
            device_id_type=MESH,
        ).start()

    def send_last_to(sub):
        send_last(sub, mine)
        each_crs(lambda core: send_last(sub, core))

    each_sub(send_last_to)
    each_crs(lambda core: send_last(me, core))
    arrived = last_rows.at[pl.ds(0, everyone - 1)]
    pltpu.make_async_copy(arrived, arrived, last_sem).wait()
    whole = jnp.broadcast_to(jnp.sum(last_rows[...], axis=0), (8, LANES)) / all_rows

    def final(d):
        return row_sum(jnp.where(lane_of == d * 4 + row_of, whole, 0.0))

    second_square = final(0)
    length_1 = jnp.sqrt(second_square / (start * start) + EPSILON)
    scale = 1.0 / (start * length_1)
    start_scale = 1.0 / start
    gram_11 = right_square * start_scale * start_scale
    gram_12 = final(1) * start_scale * scale
    gram_22 = second_square * scale * scale
    height_12 = final(2) * start_scale * scale
    height_22 = final(3) * scale * scale
    last_square = final(4) * scale * scale
    rest = (
        last_square
        - height_12 * height_12 * (2.0 - gram_11)
        - height_22 * height_22 * (2.0 - gram_22)
        + 2.0 * height_12 * height_22 * gram_12
    )
    length_2 = jnp.sqrt(jnp.maximum(rest, 0.0) + EPSILON)
    weights = least_squares(start, [[height_11, length_1], [height_12, height_22, length_2]])
    result = (weights[0] * start_scale) * first_z + (weights[1] * scale) * second_z
    following = (last * scale - (height_12 * start_scale) * right - (height_22 * scale) * second) / length_2
    for q in range(cols):
        both_ref[0, q] = result[q : q + 1]
        both_ref[1, q] = following[q : q + 1]

    for number in range(ROUNDS):
        gone = held[number].at[pl.ds(0, subs - 1)]
        pltpu.make_async_copy(gone, gone, send_sem).wait()
    for number in range(SHARES):
        gone = share.at[number, pl.ds(0, crs - 1)]
        pltpu.make_async_copy(gone, gone, share_send_sem).wait()
    pltpu.make_async_copy(arrived, arrived, last_send_sem).wait()


def body(
    right_side,
    own_block,
    coupling,
    local_inverse,
    coarse_basis,
    coarse_inverse,
    neighbours,
    margin_rows,
    block_counts,
):
    cols, rows = right_side.shape[0], right_side.shape[3]
    subs, crs = lax.axis_size("sub"), lax.axis_size("crs")
    kc = coarse_basis.shape[2]
    slots, block_rows = margin_rows.shape[2:]
    coarse_rows = crs * kc
    share_lanes = -(-coarse_rows // LANES) * LANES
    together = (LANES - 8) // kc
    groups = -(-subs // together)
    sizes = (subs, crs, cols, rows, kc, slots, share_lanes, together, groups)
    vmem = pl.BlockSpec(memory_space=pltpu.VMEM)
    stays = pl.BlockSpec(memory_space=pltpu.HBM)
    both = pl.pallas_call(
        functools.partial(kernel, sizes),
        out_shape=jax.ShapeDtypeStruct((2, cols, 1, rows), WIDE),
        in_specs=[stays] * 9,
        out_specs=vmem,
        scratch_shapes=[
            pltpu.VMEM((cols, 1, rows), WIDE),
            pltpu.VMEM((rows, rows), LOW),
            pltpu.VMEM((rows, slots * block_rows), LOW),
            pltpu.VMEM((rows, rows + slots * block_rows), LOW),
            pltpu.VMEM((1, 1, kc, rows), WIDE),
            pltpu.VMEM((coarse_rows, subs * kc), LOW),
            pltpu.SMEM((1, 1, slots), jnp.int32),
            pltpu.VMEM((1, slots, 1, block_rows), jnp.int32),
            pltpu.SMEM((1, 1, 1), jnp.int32),
            pltpu.VMEM((ROUNDS, 16, LANES), LOW),
            *[pltpu.VMEM((subs, 16, LANES), LOW) for number in range(ROUNDS)],
            pltpu.VMEM((SHARES, crs, 8, share_lanes), WIDE),
            pltpu.VMEM((subs * crs, 1, LANES), WIDE),
            pltpu.VMEM((rows, slots * block_rows), LOW),
            pltpu.VMEM((share_lanes, groups * LANES), LOW),
            pltpu.VMEM((LANES, rows), WIDE),
            pltpu.VMEM((2, LANES, rows), LOW),
            pltpu.VMEM((share_lanes, rows), WIDE),
            pltpu.VMEM((2, share_lanes, rows), LOW),
            pltpu.SemaphoreType.DMA((9,)),
            pltpu.SemaphoreType.DMA,
            pltpu.SemaphoreType.DMA((ROUNDS,)),
            pltpu.SemaphoreType.DMA,
            pltpu.SemaphoreType.DMA((SHARES,)),
            pltpu.SemaphoreType.DMA,
            pltpu.SemaphoreType.DMA,
        ],
        compiler_params=pltpu.CompilerParams(
            collective_id=0, has_side_effects=True, vmem_limit_bytes=63 * 1024 * 1024
        ),
    )(
        right_side.reshape(cols, 1, rows),
        own_block.reshape(rows, -1),
        coupling.reshape(rows, -1),
        local_inverse.reshape(rows, -1),
        coarse_basis,
        coarse_inverse.reshape(coarse_rows, -1),
        neighbours,
        margin_rows.reshape(1, slots, 1, block_rows),
        block_counts.reshape(1, 1, 1),
    )
    shape = (cols, 1, 1, rows)
    return both[0].reshape(shape), both[1].reshape(shape)


def solution(mesh):
    in_specs = (
        P(None, "sub", "crs", None),
        P("sub", "crs", None, None),
        P("sub", "crs", None, None),
        P("sub", "crs", None, None),
        P("sub", "crs", None, None),
        P("sub", None, "crs", None),
        P("sub", "crs", None),
        P("sub", "crs", None, None),
        P("sub", "crs"),
    )
    out_specs = (P(None, "sub", "crs", None), P(None, "sub", "crs", None))
    return jax.shard_map(body, mesh=mesh, in_specs=in_specs, out_specs=out_specs, check_vma=False)
```

```python
import functools

import jax
import jax.numpy as jnp
from jax import lax
from jax.experimental import pallas as pl
from jax.experimental.pallas import tpu as pltpu
from jax.sharding import PartitionSpec as P

EPSILON = 1e-06
MESH = pl.DeviceIdType.MESH
LANES = 128
ROUNDS = 4
SHARES = 2
ORDER = (15, 11, 14, 13, 10, 9, 12, 8, 7, 6, 5, 4, 3, 2, 1)
AT = 120
NT = (((1,), (1,)), ((), ()))
LOW = jnp.bfloat16
WIDE = jnp.float32


def least_squares(start_norm, columns):
    cosines = []
    sine_terms = []
    triangle = []
    target = [start_norm] + [jnp.zeros_like(start_norm) for j in range(len(columns))]
    for j, column in enumerate(columns):
        column = list(column)
        for i in range(j):
            upper_value = cosines[i] * column[i] + sine_terms[i] * column[i + 1]
            column[i + 1] = -sine_terms[i] * column[i] + cosines[i] * column[i + 1]
            column[i] = upper_value
        radius = jnp.sqrt(column[j] * column[j] + column[j + 1] * column[j + 1])
        cosine = column[j] / radius
        sine_part = column[j + 1] / radius
        column[j] = radius
        target[j + 1] = -sine_part * target[j]
        target[j] = cosine * target[j]
        cosines.append(cosine)
        sine_terms.append(sine_part)
        triangle.append(column[: j + 1])
    weights = [None] * len(columns)
    for j in reversed(range(len(columns))):
        running = target[j]
        for k in range(j + 1, len(columns)):
            running = running - triangle[k][j] * weights[k]
        weights[j] = running / triangle[j][j]
    return weights


def kernel(
    sizes,
    right_hbm,
    own_hbm,
    couple_hbm,
    inverse_hbm,
    basis_hbm,
    coarse_hbm,
    listed_hbm,
    picked_hbm,
    counts_hbm,
    both_ref,
    right_ref,
    own_ref,
    couple_ref,
    inverse_ref,
    basis_ref,
    coarse_ref,
    listed_ref,
    picked_ref,
    counts_ref,
    sent,
    held_0,
    held_1,
    held_2,
    held_3,
    share,
    last_rows,
    pick,
    coarse_wide,
    basis_parts,
    shifted,
    shifted_parts,
    load_sems,
    send_sem,
    recv_sems,
    share_send_sem,
    share_sems,
    last_send_sem,
    last_sem,
):
    subs, crs, cols, rows, kc, slots, share_lanes, together, groups = sizes
    held = (held_0, held_1, held_2, held_3)
    me = lax.axis_index("sub")
    mine = lax.axis_index("crs")
    all_rows = float(rows * subs * crs)
    row_of = lax.broadcasted_iota(jnp.int32, (8, LANES), 0)
    lane_of = lax.broadcasted_iota(jnp.int32, (8, LANES), 1)
    top = row_of < 4

    barrier = pltpu.get_barrier_semaphore()

    short = subs & (subs - 1) == 0 and subs <= 16

    def flipped(index, mask, bits):
        moved = index
        for k in range(bits):
            if mask >> k & 1:
                moved = moved + (1 << k) - (index // (1 << k)) % 2 * (2 << k)
        return moved

    def each_sub(act):
        if short:
            for mask in ORDER:
                if mask < subs:
                    act(flipped(me, mask, 4))
        else:

            def one(i, carry):
                act(lax.rem(me + i, subs))
                return carry

            lax.fori_loop(1, subs, one, 0)

    def each_crs(act):
        def one(i, carry):
            act(lax.rem(mine + i, crs))
            return carry

        if crs == 2:
            act(1 - mine)
        else:
            lax.fori_loop(1, crs, one, 0)

    def greet(sub, core):
        pl.semaphore_signal(barrier, inc=1, device_id=(sub, core), device_id_type=MESH)

    each_sub(lambda sub: greet(sub, mine))
    each_crs(lambda core: greet(me, core))

    pairs = [
        (right_hbm, right_ref),
        (basis_hbm, basis_ref),
        (picked_hbm, picked_ref),
        (counts_hbm, counts_ref),
        (coarse_hbm, coarse_ref),
        (listed_hbm, listed_ref),
        (inverse_hbm, inverse_ref),
        (own_hbm, own_ref),
        (couple_hbm, couple_ref),
    ]
    loads = [
        pltpu.make_async_copy(there, here, load_sems.at[n])
        for n, (there, here) in enumerate(pairs)
    ]
    for load in loads:
        load.start()

    def swap_halves(block):
        return pltpu.roll(block, 4, 0)

    def stack_parts(block):
        width = block.shape[1]
        high = block.astype(LOW).astype(WIDE)
        low = block - high
        at_top = lax.broadcasted_iota(jnp.int32, (8, width), 0) < 4
        return jnp.where(at_top, high, pltpu.roll(low, 4, 0)).astype(LOW)

    def nt(a, b):
        return lax.dot_general(a, b, NT, preferred_element_type=WIDE)

    def nn(a, b):
        return jnp.dot(a, b, preferred_element_type=WIDE)

    def row_sum(a):
        return jnp.sum(a, axis=1, keepdims=True)

    def restrict(block):
        both = nt(stack_parts(block), basis_parts[...])
        both = both + pltpu.roll(both, LANES // 2, 1)
        both = jnp.where(lane_of < kc, both + swap_halves(both), 0.0)
        moved = both
        for t in range(1, together):
            moved = jnp.where(lax.rem(me, together) == t, pltpu.roll(both, t * kc, 1), moved)
        return moved

    def encode(value):
        high = value.astype(LOW).astype(WIDE)
        rest = value - high
        middle = rest.astype(LOW).astype(WIDE)
        low = rest - middle
        spread = jnp.where(lane_of == AT, high, 0.0)
        spread = jnp.where(lane_of == AT + 1, middle, spread)
        return jnp.where(lane_of == AT + 2, low, spread)

    def pack(block, extra):
        first = jnp.where(top, block[:, :LANES], swap_halves(block[:, LANES : 2 * LANES]))
        second = jnp.where(top, block[:, 2 * LANES :], swap_halves(extra))
        return jnp.concatenate([first, second], axis=0).astype(LOW)

    def send(number, tile):
        sent[number] = tile

        def one(sub):
            pltpu.make_async_remote_copy(
                src_ref=sent.at[number],
                dst_ref=held[number].at[me],
                send_sem=send_sem,
                recv_sem=recv_sems.at[number],
                device_id=(sub, mine),
                device_id_type=MESH,
            ).start()

        each_sub(one)

    def receive(number):
        arrived = held[number].at[pl.ds(0, subs - 1)]
        pltpu.make_async_copy(arrived, arrived, recv_sems.at[number]).wait()

    def send_share(number, block):
        share[number, mine] = block

        def one(core):
            pltpu.make_async_remote_copy(
                src_ref=share.at[number, mine],
                dst_ref=share.at[number, mine],
                send_sem=share_send_sem,
                recv_sem=share_sems.at[number],
                device_id=(me, core),
                device_id_type=MESH,
            ).start()

        each_crs(one)

    def receive_share(number):
        arrived = share.at[number, pl.ds(0, crs - 1)]
        pltpu.make_async_copy(arrived, arrived, share_sems.at[number]).wait()
        total = share[number, 0]
        for c in range(1, crs):
            total = total + share[number, c]
        return total

    def fetch(number):
        lines = []
        for j in range(slots):
            tile = held[number][listed_ref[0, 0, j]].astype(WIDE)
            first = tile[:8]
            lines.append(jnp.concatenate([first, swap_halves(first), tile[8:]], axis=1))
        return nn(jnp.concatenate(lines, axis=0).astype(LOW), pick[...])

    def margin(fetched):
        parts = [
            fetched[8 * j : 8 * j + 8, LANES * j : LANES * j + LANES] for j in range(slots)
        ]
        return jnp.concatenate(parts, axis=1).astype(LOW)

    def group_sums(number):
        sums = []
        for g in range(groups):
            members = range(g * together, min(subs, (g + 1) * together))
            tiles = [held[number][s].astype(WIDE)[8:] for s in members]
            sums.append(functools.reduce(jnp.add, tiles))
        return sums

    def with_scalars(solved, totals):
        if share_lanes > LANES:
            totals = jnp.concatenate(
                [totals, jnp.zeros((8, share_lanes - LANES), WIDE)], axis=1
            )
        at_top = lax.broadcasted_iota(jnp.int32, (8, share_lanes), 0) < 4
        return jnp.where(at_top, pltpu.roll(solved, 4, 0), totals)

    def scalar(block):
        return row_sum(jnp.where((lane_of >= AT) & (lane_of < AT + 3), block, 0.0))

    def prolong(total):
        parts = stack_parts(total)
        both = nn(jnp.concatenate([parts, parts], axis=1), shifted_parts[...])
        return both + pltpu.roll(both, 4, 0)

    def precondition(number, share_number, own_part):
        receive(number)
        sums = group_sums(number)
        solved = nt(jnp.concatenate(sums, axis=1).astype(LOW), coarse_wide[...])
        fetched = fetch(number)
        totals = functools.reduce(jnp.add, sums)
        send_share(share_number, with_scalars(solved, totals))
        fine = own_part + nt(margin(fetched), inverse_ref[:, rows:])
        total = receive_share(share_number)
        return fine + prolong(total), swap_halves(total[:, :LANES])

    loads[0].wait()
    loads[1].wait()
    right = jnp.concatenate(
        [right_ref[q] for q in range(cols)] + [jnp.zeros((8 - cols, rows), WIDE)], axis=0
    )
    basis = basis_ref[0, 0]
    basis_high = basis.astype(LOW).astype(WIDE)
    gap = jnp.zeros((LANES // 2 - kc, rows), WIDE)
    basis_parts[...] = jnp.concatenate(
        [basis_high, gap, basis - basis_high, gap], axis=0
    ).astype(LOW)
    extra = restrict(right) + encode(row_sum(right * right))
    tile = pack(right, extra)
    held_0[me] = tile
    pl.semaphore_wait(barrier, subs - 1 + crs - 1)
    send(0, tile)

    loads[2].wait()
    loads[3].wait()
    live = lax.broadcasted_iota(jnp.int32, (slots, LANES), 0) < counts_ref[0, 0, 0]
    wanted = jnp.where(
        live, jnp.concatenate([picked_ref[0, j] for j in range(slots)], axis=0), -1
    )
    row_index = lax.broadcasted_iota(jnp.int32, (rows, LANES), 0)
    for j in range(slots):
        pick[:, j * LANES : (j + 1) * LANES] = jnp.where(
            row_index == wanted[j : j + 1], 1.0, 0.0
        ).astype(LOW)
    shifted[...] = jnp.zeros_like(shifted)
    shifted[pl.ds(pl.multiple_of(mine * kc, 8), kc), :] = basis
    shifted_full = shifted[...]
    shifted_high = shifted_full.astype(LOW)
    shifted_parts[:share_lanes] = shifted_high
    shifted_parts[share_lanes:] = (shifted_full - shifted_high.astype(WIDE)).astype(LOW)
    loads[4].wait()
    coarse_rows = crs * kc
    coarse_cols = subs * kc
    coarse_wide[...] = jnp.zeros_like(coarse_wide)
    coarse_lane = lax.broadcasted_iota(jnp.int32, (coarse_rows, LANES), 1)
    for g in range(groups):
        first = g * together * kc
        count = min(together * kc, coarse_cols - first)
        base = first // LANES * LANES
        offset = first - base
        width = LANES if offset + count <= LANES else 2 * LANES
        window = coarse_ref[:, base : base + width].astype(WIDE)
        if offset:
            window = pltpu.roll(window, width - offset, 1)
        coarse_wide[:coarse_rows, g * LANES : (g + 1) * LANES] = jnp.where(
            coarse_lane < count, window[:, :LANES], 0.0
        ).astype(LOW)
    loads[5].wait()
    loads[6].wait()
    own_fine = nt(right.astype(LOW), inverse_ref[:, :rows])

    first_z, totals = precondition(0, 0, own_fine)
    right_square = scalar(totals) / all_rows
    start = jnp.sqrt(right_square + EPSILON)

    nothing = jnp.zeros((8, LANES), WIDE)
    send(1, pack(first_z, nothing))
    loads[7].wait()
    loads[8].wait()
    own_part = nt(first_z.astype(LOW), own_ref[...])
    receive(1)
    mapped = own_part + nt(margin(fetch(1)), couple_ref[...])

    extra = restrict(mapped) + encode(row_sum(mapped * right))
    tile = pack(mapped, extra)
    held_2[me] = tile
    send(2, tile)
    own_fine = nt(mapped.astype(LOW), inverse_ref[:, :rows])
    mapped_z, totals = precondition(2, 1, own_fine)
    height_11 = scalar(totals) / all_rows / (start * start)
    second_z = mapped_z - height_11 * first_z
    second = mapped - height_11 * right

    send(3, pack(second_z, nothing))
    own_part = nt(second_z.astype(LOW), own_ref[...])
    products = [row_sum(second * second), row_sum(right * second)]
    receive(3)
    last = own_part + nt(margin(fetch(3)), couple_ref[...])

    products = products + [row_sum(last * right), row_sum(last * second), row_sum(last * last)]
    line = jnp.zeros((8, LANES), WIDE)
    for d, value in enumerate(products):
        line = jnp.where((lane_of == d * 4 + row_of) & top, value, line)
    here = me * crs + mine
    everyone = subs * crs
    last_rows[here] = jnp.sum(line, axis=0, keepdims=True)

    def send_last(sub, core):
        pltpu.make_async_remote_copy(
            src_ref=last_rows.at[here],
            dst_ref=last_rows.at[here],
            send_sem=last_send_sem,
            recv_sem=last_sem,
            device_id=(sub, core),
            device_id_type=MESH,
        ).start()

    def send_last_to(sub):
        send_last(sub, mine)
        each_crs(lambda core: send_last(sub, core))

    each_sub(send_last_to)
    each_crs(lambda core: send_last(me, core))
    arrived = last_rows.at[pl.ds(0, everyone - 1)]
    pltpu.make_async_copy(arrived, arrived, last_sem).wait()
    whole = jnp.broadcast_to(jnp.sum(last_rows[...], axis=0), (8, LANES)) / all_rows

    def final(d):
        return row_sum(jnp.where(lane_of == d * 4 + row_of, whole, 0.0))

    second_square = final(0)
    length_1 = jnp.sqrt(second_square / (start * start) + EPSILON)
    scale = 1.0 / (start * length_1)
    start_scale = 1.0 / start
    gram_11 = right_square * start_scale * start_scale
    gram_12 = final(1) * start_scale * scale
    gram_22 = second_square * scale * scale
    height_12 = final(2) * start_scale * scale
    height_22 = final(3) * scale * scale
    last_square = final(4) * scale * scale
    rest = (
        last_square
        - height_12 * height_12 * (2.0 - gram_11)
        - height_22 * height_22 * (2.0 - gram_22)
        + 2.0 * height_12 * height_22 * gram_12
    )
    length_2 = jnp.sqrt(jnp.maximum(rest, 0.0) + EPSILON)
    weights = least_squares(start, [[height_11, length_1], [height_12, height_22, length_2]])
    result = (weights[0] * start_scale) * first_z + (weights[1] * scale) * second_z
    following = (last * scale - (height_12 * start_scale) * right - (height_22 * scale) * second) / length_2
    for q in range(cols):
        both_ref[0, q] = result[q : q + 1]
        both_ref[1, q] = following[q : q + 1]

    for number in range(ROUNDS):
        gone = held[number].at[pl.ds(0, subs - 1)]
        pltpu.make_async_copy(gone, gone, send_sem).wait()
    for number in range(SHARES):
        gone = share.at[number, pl.ds(0, crs - 1)]
        pltpu.make_async_copy(gone, gone, share_send_sem).wait()
    pltpu.make_async_copy(arrived, arrived, last_send_sem).wait()


def body(
    right_side,
    own_block,
    coupling,
    local_inverse,
    coarse_basis,
    coarse_inverse,
    neighbours,
    margin_rows,
    block_counts,
):
    cols, rows = right_side.shape[0], right_side.shape[3]
    subs, crs = lax.axis_size("sub"), lax.axis_size("crs")
    kc = coarse_basis.shape[2]
    slots, block_rows = margin_rows.shape[2:]
    coarse_rows = crs * kc
    share_lanes = -(-coarse_rows // LANES) * LANES
    together = (LANES - 8) // kc
    groups = -(-subs // together)
    sizes = (subs, crs, cols, rows, kc, slots, share_lanes, together, groups)
    vmem = pl.BlockSpec(memory_space=pltpu.VMEM)
    stays = pl.BlockSpec(memory_space=pltpu.HBM)
    both = pl.pallas_call(
        functools.partial(kernel, sizes),
        out_shape=pltpu.VMEM((2, cols, 1, rows), WIDE),
        in_specs=[stays] * 9,
        out_specs=vmem,
        scratch_shapes=[
            pltpu.VMEM((cols, 1, rows), WIDE),
            pltpu.VMEM((rows, rows), LOW),
            pltpu.VMEM((rows, slots * block_rows), LOW),
            pltpu.VMEM((rows, rows + slots * block_rows), LOW),
            pltpu.VMEM((1, 1, kc, rows), WIDE),
            pltpu.VMEM((coarse_rows, subs * kc), LOW),
            pltpu.SMEM((1, 1, slots), jnp.int32),
            pltpu.VMEM((1, slots, 1, block_rows), jnp.int32),
            pltpu.SMEM((1, 1, 1), jnp.int32),
            pltpu.VMEM((ROUNDS, 16, LANES), LOW),
            *[pltpu.VMEM((subs, 16, LANES), LOW) for number in range(ROUNDS)],
            pltpu.VMEM((SHARES, crs, 8, share_lanes), WIDE),
            pltpu.VMEM((subs * crs, 1, LANES), WIDE),
            pltpu.VMEM((rows, slots * block_rows), LOW),
            pltpu.VMEM((share_lanes, groups * LANES), LOW),
            pltpu.VMEM((LANES, rows), LOW),
            pltpu.VMEM((share_lanes, rows), WIDE),
            pltpu.VMEM((2 * share_lanes, rows), LOW),
            pltpu.SemaphoreType.DMA((9,)),
            pltpu.SemaphoreType.DMA,
            pltpu.SemaphoreType.DMA((ROUNDS,)),
            pltpu.SemaphoreType.DMA,
            pltpu.SemaphoreType.DMA((SHARES,)),
            pltpu.SemaphoreType.DMA,
            pltpu.SemaphoreType.DMA,
        ],
        compiler_params=pltpu.CompilerParams(
            collective_id=0, has_side_effects=True, vmem_limit_bytes=63 * 1024 * 1024
        ),
    )(
        right_side.reshape(cols, 1, rows),
        own_block.reshape(rows, -1),
        coupling.reshape(rows, -1),
        local_inverse.reshape(rows, -1),
        coarse_basis,
        coarse_inverse.reshape(coarse_rows, -1),
        neighbours,
        margin_rows.reshape(1, slots, 1, block_rows),
        block_counts.reshape(1, 1, 1),
    )
    shape = (cols, 1, 1, rows)
    return both[0].reshape(shape), both[1].reshape(shape)


def solution(mesh):
    in_specs = (
        P(None, "sub", "crs", None),
        P("sub", "crs", None, None),
        P("sub", "crs", None, None),
        P("sub", "crs", None, None),
        P("sub", "crs", None, None),
        P("sub", None, "crs", None),
        P("sub", "crs", None),
        P("sub", "crs", None, None),
        P("sub", "crs"),
    )
    out_specs = (P(None, "sub", "crs", None), P(None, "sub", "crs", None))
    return jax.shard_map(body, mesh=mesh, in_specs=in_specs, out_specs=out_specs, check_vma=False)
```

```python
import functools

import jax
import jax.numpy as jnp
from jax import lax
from jax.experimental import pallas as pl
from jax.experimental.pallas import tpu as pltpu
from jax.sharding import PartitionSpec as P

EPSILON = 1e-06
MESH = pl.DeviceIdType.MESH
LANES = 128
ROUNDS = 4
SHARES = 2
ORDER = (15, 11, 14, 13, 10, 9, 12, 8, 7, 6, 5, 4, 3, 2, 1)
AT = 120
NT = (((1,), (1,)), ((), ()))
LOW = jnp.bfloat16
WIDE = jnp.float32


def least_squares(start_norm, columns):
    cosines = []
    sine_terms = []
    triangle = []
    target = [start_norm] + [jnp.zeros_like(start_norm) for j in range(len(columns))]
    for j, column in enumerate(columns):
        column = list(column)
        for i in range(j):
            upper_value = cosines[i] * column[i] + sine_terms[i] * column[i + 1]
            column[i + 1] = -sine_terms[i] * column[i] + cosines[i] * column[i + 1]
            column[i] = upper_value
        radius = jnp.sqrt(column[j] * column[j] + column[j + 1] * column[j + 1])
        cosine = column[j] / radius
        sine_part = column[j + 1] / radius
        column[j] = radius
        target[j + 1] = -sine_part * target[j]
        target[j] = cosine * target[j]
        cosines.append(cosine)
        sine_terms.append(sine_part)
        triangle.append(column[: j + 1])
    weights = [None] * len(columns)
    for j in reversed(range(len(columns))):
        running = target[j]
        for k in range(j + 1, len(columns)):
            running = running - triangle[k][j] * weights[k]
        weights[j] = running / triangle[j][j]
    return weights


def kernel(
    sizes,
    right_hbm,
    own_hbm,
    couple_hbm,
    inverse_hbm,
    basis_hbm,
    coarse_hbm,
    listed_hbm,
    picked_hbm,
    counts_hbm,
    both_ref,
    right_ref,
    own_ref,
    couple_ref,
    inverse_ref,
    basis_ref,
    coarse_ref,
    listed_ref,
    picked_ref,
    counts_ref,
    sent,
    held_0,
    held_1,
    held_2,
    held_3,
    share,
    last_rows,
    own_t,
    couple_t,
    inverse_t,
    pick,
    coarse_wide,
    basis_parts,
    shifted,
    shifted_parts,
    load_sems,
    send_sem,
    recv_sems,
    share_send_sem,
    share_sems,
    last_send_sem,
    last_sem,
):
    subs, crs, cols, rows, kc, slots, share_lanes, together, groups = sizes
    held = (held_0, held_1, held_2, held_3)
    me = lax.axis_index("sub")
    mine = lax.axis_index("crs")
    all_rows = float(rows * subs * crs)
    row_of = lax.broadcasted_iota(jnp.int32, (8, LANES), 0)
    lane_of = lax.broadcasted_iota(jnp.int32, (8, LANES), 1)
    top = row_of < 4

    barrier = pltpu.get_barrier_semaphore()

    short = subs & (subs - 1) == 0 and subs <= 16

    def flipped(index, mask, bits):
        moved = index
        for k in range(bits):
            if mask >> k & 1:
                moved = moved + (1 << k) - (index // (1 << k)) % 2 * (2 << k)
        return moved

    def each_sub(act):
        if short:
            for mask in ORDER:
                if mask < subs:
                    act(flipped(me, mask, 4))
        else:

            def one(i, carry):
                act(lax.rem(me + i, subs))
                return carry

            lax.fori_loop(1, subs, one, 0)

    def each_crs(act):
        def one(i, carry):
            act(lax.rem(mine + i, crs))
            return carry

        if crs == 2:
            act(1 - mine)
        else:
            lax.fori_loop(1, crs, one, 0)

    def greet(sub, core):
        pl.semaphore_signal(barrier, inc=1, device_id=(sub, core), device_id_type=MESH)

    each_sub(lambda sub: greet(sub, mine))
    each_crs(lambda core: greet(me, core))

    pairs = [
        (right_hbm, right_ref),
        (basis_hbm, basis_ref),
        (picked_hbm, picked_ref),
        (counts_hbm, counts_ref),
        (coarse_hbm, coarse_ref),
        (listed_hbm, listed_ref),
        (inverse_hbm, inverse_ref),
        (own_hbm, own_ref),
        (couple_hbm, couple_ref),
    ]
    loads = [
        pltpu.make_async_copy(there, here, load_sems.at[n])
        for n, (there, here) in enumerate(pairs)
    ]
    for load in loads:
        load.start()

    def swap_halves(block):
        return pltpu.roll(block, 4, 0)

    def stack_parts(block):
        width = block.shape[1]
        high = block.astype(LOW).astype(WIDE)
        low = block - high
        at_top = lax.broadcasted_iota(jnp.int32, (8, width), 0) < 4
        return jnp.where(at_top, high, pltpu.roll(low, 4, 0)).astype(LOW)

    def nt(a, b):
        return lax.dot_general(a, b, NT, preferred_element_type=WIDE)

    def nn(a, b):
        return jnp.dot(a, b, preferred_element_type=WIDE)

    def turn(source, target):
        for k in range(0, source.shape[1], LANES):
            target[k : k + LANES, :] = source[:, k : k + LANES].T

    def row_sum(a):
        return jnp.sum(a, axis=1, keepdims=True)

    def restrict(block):
        both = nt(stack_parts(block), basis_parts[...])
        both = both + pltpu.roll(both, LANES // 2, 1)
        both = jnp.where(lane_of < kc, both + swap_halves(both), 0.0)
        moved = both
        for t in range(1, together):
            moved = jnp.where(lax.rem(me, together) == t, pltpu.roll(both, t * kc, 1), moved)
        return moved

    def encode(value):
        high = value.astype(LOW).astype(WIDE)
        rest = value - high
        middle = rest.astype(LOW).astype(WIDE)
        low = rest - middle
        spread = jnp.where(lane_of == AT, high, 0.0)
        spread = jnp.where(lane_of == AT + 1, middle, spread)
        return jnp.where(lane_of == AT + 2, low, spread)

    def pack(block, extra):
        first = jnp.where(top, block[:, :LANES], swap_halves(block[:, LANES : 2 * LANES]))
        second = jnp.where(top, block[:, 2 * LANES :], swap_halves(extra))
        return jnp.concatenate([first, second], axis=0).astype(LOW)

    def send(number, tile):
        sent[number] = tile

        def one(sub):
            pltpu.make_async_remote_copy(
                src_ref=sent.at[number],
                dst_ref=held[number].at[me],
                send_sem=send_sem,
                recv_sem=recv_sems.at[number],
                device_id=(sub, mine),
                device_id_type=MESH,
            ).start()

        each_sub(one)

    def receive(number):
        arrived = held[number].at[pl.ds(0, subs - 1)]
        pltpu.make_async_copy(arrived, arrived, recv_sems.at[number]).wait()

    def send_share(number, block):
        share[number, mine] = block

        def one(core):
            pltpu.make_async_remote_copy(
                src_ref=share.at[number, mine],
                dst_ref=share.at[number, mine],
                send_sem=share_send_sem,
                recv_sem=share_sems.at[number],
                device_id=(me, core),
                device_id_type=MESH,
            ).start()

        each_crs(one)

    def receive_share(number):
        arrived = share.at[number, pl.ds(0, crs - 1)]
        pltpu.make_async_copy(arrived, arrived, share_sems.at[number]).wait()
        total = share[number, 0]
        for c in range(1, crs):
            total = total + share[number, c]
        return total

    def fetch(number):
        lines = []
        for j in range(slots):
            tile = held[number][listed_ref[0, 0, j]].astype(WIDE)
            first = tile[:8]
            lines.append(jnp.concatenate([first, swap_halves(first), tile[8:]], axis=1))
        return nn(jnp.concatenate(lines, axis=0).astype(LOW), pick[...])

    def margin(fetched):
        parts = [
            fetched[8 * j : 8 * j + 8, LANES * j : LANES * j + LANES] for j in range(slots)
        ]
        return jnp.concatenate(parts, axis=1).astype(LOW)

    def group_sums(number):
        sums = []
        for g in range(groups):
            members = range(g * together, min(subs, (g + 1) * together))
            tiles = [held[number][s].astype(WIDE)[8:] for s in members]
            sums.append(functools.reduce(jnp.add, tiles))
        return sums

    def with_scalars(solved, totals):
        if share_lanes > LANES:
            totals = jnp.concatenate(
                [totals, jnp.zeros((8, share_lanes - LANES), WIDE)], axis=1
            )
        at_top = lax.broadcasted_iota(jnp.int32, (8, share_lanes), 0) < 4
        return jnp.where(at_top, pltpu.roll(solved, 4, 0), totals)

    def scalar(block):
        return row_sum(jnp.where((lane_of >= AT) & (lane_of < AT + 3), block, 0.0))

    def prolong(total):
        parts = stack_parts(total)
        both = nn(jnp.concatenate([parts, parts], axis=1), shifted_parts[...])
        return both + pltpu.roll(both, 4, 0)

    def precondition(number, share_number, own_part):
        receive(number)
        sums = group_sums(number)
        solved = nt(jnp.concatenate(sums, axis=1).astype(LOW), coarse_wide[...])
        fetched = fetch(number)
        totals = functools.reduce(jnp.add, sums)
        send_share(share_number, with_scalars(solved, totals))
        fine = own_part + nn(margin(fetched), inverse_t[rows:])
        total = receive_share(share_number)
        return fine + prolong(total), swap_halves(total[:, :LANES])

    loads[0].wait()
    loads[1].wait()
    right = jnp.concatenate(
        [right_ref[q] for q in range(cols)] + [jnp.zeros((8 - cols, rows), WIDE)], axis=0
    )
    basis = basis_ref[0, 0]
    basis_high = basis.astype(LOW).astype(WIDE)
    gap = jnp.zeros((LANES // 2 - kc, rows), WIDE)
    basis_parts[...] = jnp.concatenate(
        [basis_high, gap, basis - basis_high, gap], axis=0
    ).astype(LOW)
    extra = restrict(right) + encode(row_sum(right * right))
    tile = pack(right, extra)
    held_0[me] = tile
    pl.semaphore_wait(barrier, subs - 1 + crs - 1)
    send(0, tile)

    loads[2].wait()
    loads[3].wait()
    live = lax.broadcasted_iota(jnp.int32, (slots, LANES), 0) < counts_ref[0, 0, 0]
    wanted = jnp.where(
        live, jnp.concatenate([picked_ref[0, j] for j in range(slots)], axis=0), -1
    )
    row_index = lax.broadcasted_iota(jnp.int32, (rows, LANES), 0)
    for j in range(slots):
        pick[:, j * LANES : (j + 1) * LANES] = jnp.where(
            row_index == wanted[j : j + 1], 1.0, 0.0
        ).astype(LOW)
    shifted[...] = jnp.zeros_like(shifted)
    shifted[pl.ds(pl.multiple_of(mine * kc, 8), kc), :] = basis
    shifted_full = shifted[...]
    shifted_high = shifted_full.astype(LOW)
    shifted_parts[:share_lanes] = shifted_high
    shifted_parts[share_lanes:] = (shifted_full - shifted_high.astype(WIDE)).astype(LOW)
    loads[4].wait()
    coarse_rows = crs * kc
    coarse_cols = subs * kc
    coarse_wide[...] = jnp.zeros_like(coarse_wide)
    coarse_lane = lax.broadcasted_iota(jnp.int32, (coarse_rows, LANES), 1)
    for g in range(groups):
        first = g * together * kc
        count = min(together * kc, coarse_cols - first)
        base = first // LANES * LANES
        offset = first - base
        width = LANES if offset + count <= LANES else 2 * LANES
        window = coarse_ref[:, base : base + width].astype(WIDE)
        if offset:
            window = pltpu.roll(window, width - offset, 1)
        coarse_wide[:coarse_rows, g * LANES : (g + 1) * LANES] = jnp.where(
            coarse_lane < count, window[:, :LANES], 0.0
        ).astype(LOW)
    loads[5].wait()
    loads[6].wait()
    turn(inverse_ref, inverse_t)
    own_fine = nn(right.astype(LOW), inverse_t[:rows])

    first_z, totals = precondition(0, 0, own_fine)
    right_square = scalar(totals) / all_rows
    start = jnp.sqrt(right_square + EPSILON)

    nothing = jnp.zeros((8, LANES), WIDE)
    send(1, pack(first_z, nothing))
    loads[7].wait()
    loads[8].wait()
    turn(own_ref, own_t)
    turn(couple_ref, couple_t)
    own_part = nn(first_z.astype(LOW), own_t[...])
    receive(1)
    mapped = own_part + nn(margin(fetch(1)), couple_t[...])

    extra = restrict(mapped) + encode(row_sum(mapped * right))
    tile = pack(mapped, extra)
    held_2[me] = tile
    send(2, tile)
    own_fine = nn(mapped.astype(LOW), inverse_t[:rows])
    mapped_z, totals = precondition(2, 1, own_fine)
    height_11 = scalar(totals) / all_rows / (start * start)
    second_z = mapped_z - height_11 * first_z
    second = mapped - height_11 * right

    send(3, pack(second_z, nothing))
    own_part = nn(second_z.astype(LOW), own_t[...])
    products = [row_sum(second * second), row_sum(right * second)]
    receive(3)
    last = own_part + nn(margin(fetch(3)), couple_t[...])

    products = products + [row_sum(last * right), row_sum(last * second), row_sum(last * last)]
    line = jnp.zeros((8, LANES), WIDE)
    for d, value in enumerate(products):
        line = jnp.where((lane_of == d * 4 + row_of) & top, value, line)
    here = me * crs + mine
    everyone = subs * crs
    last_rows[here] = jnp.sum(line, axis=0, keepdims=True)

    def send_last(sub, core):
        pltpu.make_async_remote_copy(
            src_ref=last_rows.at[here],
            dst_ref=last_rows.at[here],
            send_sem=last_send_sem,
            recv_sem=last_sem,
            device_id=(sub, core),
            device_id_type=MESH,
        ).start()

    def send_last_to(sub):
        send_last(sub, mine)
        each_crs(lambda core: send_last(sub, core))

    each_sub(send_last_to)
    each_crs(lambda core: send_last(me, core))
    arrived = last_rows.at[pl.ds(0, everyone - 1)]
    pltpu.make_async_copy(arrived, arrived, last_sem).wait()
    whole = jnp.broadcast_to(jnp.sum(last_rows[...], axis=0), (8, LANES)) / all_rows

    def final(d):
        return row_sum(jnp.where(lane_of == d * 4 + row_of, whole, 0.0))

    second_square = final(0)
    length_1 = jnp.sqrt(second_square / (start * start) + EPSILON)
    scale = 1.0 / (start * length_1)
    start_scale = 1.0 / start
    gram_11 = right_square * start_scale * start_scale
    gram_12 = final(1) * start_scale * scale
    gram_22 = second_square * scale * scale
    height_12 = final(2) * start_scale * scale
    height_22 = final(3) * scale * scale
    last_square = final(4) * scale * scale
    rest = (
        last_square
        - height_12 * height_12 * (2.0 - gram_11)
        - height_22 * height_22 * (2.0 - gram_22)
        + 2.0 * height_12 * height_22 * gram_12
    )
    length_2 = jnp.sqrt(jnp.maximum(rest, 0.0) + EPSILON)
    weights = least_squares(start, [[height_11, length_1], [height_12, height_22, length_2]])
    result = (weights[0] * start_scale) * first_z + (weights[1] * scale) * second_z
    following = (last * scale - (height_12 * start_scale) * right - (height_22 * scale) * second) / length_2
    for q in range(cols):
        both_ref[0, q] = result[q : q + 1]
        both_ref[1, q] = following[q : q + 1]

    for number in range(ROUNDS):
        gone = held[number].at[pl.ds(0, subs - 1)]
        pltpu.make_async_copy(gone, gone, send_sem).wait()
    for number in range(SHARES):
        gone = share.at[number, pl.ds(0, crs - 1)]
        pltpu.make_async_copy(gone, gone, share_send_sem).wait()
    pltpu.make_async_copy(arrived, arrived, last_send_sem).wait()


def body(
    right_side,
    own_block,
    coupling,
    local_inverse,
    coarse_basis,
    coarse_inverse,
    neighbours,
    margin_rows,
    block_counts,
):
    cols, rows = right_side.shape[0], right_side.shape[3]
    subs, crs = lax.axis_size("sub"), lax.axis_size("crs")
    kc = coarse_basis.shape[2]
    slots, block_rows = margin_rows.shape[2:]
    coarse_rows = crs * kc
    share_lanes = -(-coarse_rows // LANES) * LANES
    together = (LANES - 8) // kc
    groups = -(-subs // together)
    sizes = (subs, crs, cols, rows, kc, slots, share_lanes, together, groups)
    vmem = pl.BlockSpec(memory_space=pltpu.VMEM)
    stays = pl.BlockSpec(memory_space=pltpu.HBM)
    both = pl.pallas_call(
        functools.partial(kernel, sizes),
        out_shape=pltpu.VMEM((2, cols, 1, rows), WIDE),
        in_specs=[stays] * 9,
        out_specs=vmem,
        scratch_shapes=[
            pltpu.VMEM((cols, 1, rows), WIDE),
            pltpu.VMEM((rows, rows), LOW),
            pltpu.VMEM((rows, slots * block_rows), LOW),
            pltpu.VMEM((rows, rows + slots * block_rows), LOW),
            pltpu.VMEM((1, 1, kc, rows), WIDE),
            pltpu.VMEM((coarse_rows, subs * kc), LOW),
            pltpu.SMEM((1, 1, slots), jnp.int32),
            pltpu.VMEM((1, slots, 1, block_rows), jnp.int32),
            pltpu.SMEM((1, 1, 1), jnp.int32),
            pltpu.VMEM((ROUNDS, 16, LANES), LOW),
            *[pltpu.VMEM((subs, 16, LANES), LOW) for number in range(ROUNDS)],
            pltpu.VMEM((SHARES, crs, 8, share_lanes), WIDE),
            pltpu.VMEM((subs * crs, 1, LANES), WIDE),
            pltpu.VMEM((rows, rows), LOW),
            pltpu.VMEM((slots * block_rows, rows), LOW),
            pltpu.VMEM((rows + slots * block_rows, rows), LOW),
            pltpu.VMEM((rows, slots * block_rows), LOW),
            pltpu.VMEM((share_lanes, groups * LANES), LOW),
            pltpu.VMEM((LANES, rows), LOW),
            pltpu.VMEM((share_lanes, rows), WIDE),
            pltpu.VMEM((2 * share_lanes, rows), LOW),
            pltpu.SemaphoreType.DMA((9,)),
            pltpu.SemaphoreType.DMA,
            pltpu.SemaphoreType.DMA((ROUNDS,)),
            pltpu.SemaphoreType.DMA,
            pltpu.SemaphoreType.DMA((SHARES,)),
            pltpu.SemaphoreType.DMA,
            pltpu.SemaphoreType.DMA,
        ],
        compiler_params=pltpu.CompilerParams(
            collective_id=0, has_side_effects=True, vmem_limit_bytes=63 * 1024 * 1024
        ),
    )(
        right_side.reshape(cols, 1, rows),
        own_block.reshape(rows, -1),
        coupling.reshape(rows, -1),
        local_inverse.reshape(rows, -1),
        coarse_basis,
        coarse_inverse.reshape(coarse_rows, -1),
        neighbours,
        margin_rows.reshape(1, slots, 1, block_rows),
        block_counts.reshape(1, 1, 1),
    )
    shape = (cols, 1, 1, rows)
    return both[0].reshape(shape), both[1].reshape(shape)


def solution(mesh):
    in_specs = (
        P(None, "sub", "crs", None),
        P("sub", "crs", None, None),
        P("sub", "crs", None, None),
        P("sub", "crs", None, None),
        P("sub", "crs", None, None),
        P("sub", None, "crs", None),
        P("sub", "crs", None),
        P("sub", "crs", None, None),
        P("sub", "crs"),
    )
    out_specs = (P(None, "sub", "crs", None), P(None, "sub", "crs", None))
    return jax.shard_map(body, mesh=mesh, in_specs=in_specs, out_specs=out_specs, check_vma=False)
```

```python
import functools

import jax
import jax.numpy as jnp
from jax import lax
from jax.experimental import pallas as pl
from jax.experimental.pallas import tpu as pltpu
from jax.sharding import PartitionSpec as P

EPSILON = 1e-06
MESH = pl.DeviceIdType.MESH
LANES = 128
ROUNDS = 4
SHARES = 2
ORDER = (15, 11, 14, 13, 10, 9, 12, 8, 7, 6, 5, 4, 3, 2, 1)
AT = 120
NT = (((1,), (1,)), ((), ()))
LOW = jnp.bfloat16
WIDE = jnp.float32


def least_squares(start_norm, columns):
    cosines = []
    sine_terms = []
    triangle = []
    target = [start_norm] + [jnp.zeros_like(start_norm) for j in range(len(columns))]
    for j, column in enumerate(columns):
        column = list(column)
        for i in range(j):
            upper_value = cosines[i] * column[i] + sine_terms[i] * column[i + 1]
            column[i + 1] = -sine_terms[i] * column[i] + cosines[i] * column[i + 1]
            column[i] = upper_value
        radius = jnp.sqrt(column[j] * column[j] + column[j + 1] * column[j + 1])
        cosine = column[j] / radius
        sine_part = column[j + 1] / radius
        column[j] = radius
        target[j + 1] = -sine_part * target[j]
        target[j] = cosine * target[j]
        cosines.append(cosine)
        sine_terms.append(sine_part)
        triangle.append(column[: j + 1])
    weights = [None] * len(columns)
    for j in reversed(range(len(columns))):
        running = target[j]
        for k in range(j + 1, len(columns)):
            running = running - triangle[k][j] * weights[k]
        weights[j] = running / triangle[j][j]
    return weights


def kernel(
    sizes,
    right_hbm,
    own_hbm,
    couple_hbm,
    inverse_hbm,
    basis_hbm,
    coarse_hbm,
    listed_hbm,
    picked_hbm,
    counts_hbm,
    both_ref,
    right_ref,
    own_ref,
    couple_ref,
    inverse_ref,
    basis_ref,
    coarse_ref,
    listed_ref,
    picked_ref,
    counts_ref,
    sent,
    held_0,
    held_1,
    held_2,
    held_3,
    share,
    last_rows,
    own_t,
    couple_wide,
    inverse_t,
    pick,
    coarse_wide,
    basis_parts,
    shifted,
    shifted_parts,
    load_sems,
    send_sem,
    recv_sems,
    share_send_sem,
    share_sems,
    last_send_sem,
    last_sem,
):
    subs, crs, cols, rows, kc, slots, share_lanes, together, groups = sizes
    held = (held_0, held_1, held_2, held_3)
    me = lax.axis_index("sub")
    mine = lax.axis_index("crs")
    all_rows = float(rows * subs * crs)
    row_of = lax.broadcasted_iota(jnp.int32, (8, LANES), 0)
    lane_of = lax.broadcasted_iota(jnp.int32, (8, LANES), 1)
    top = row_of < 4

    barrier = pltpu.get_barrier_semaphore()

    short = subs & (subs - 1) == 0 and subs <= 16

    def flipped(index, mask, bits):
        moved = index
        for k in range(bits):
            if mask >> k & 1:
                moved = moved + (1 << k) - (index // (1 << k)) % 2 * (2 << k)
        return moved

    def each_sub(act):
        if short:
            for mask in ORDER:
                if mask < subs:
                    act(flipped(me, mask, 4))
        else:

            def one(i, carry):
                act(lax.rem(me + i, subs))
                return carry

            lax.fori_loop(1, subs, one, 0)

    def each_crs(act):
        def one(i, carry):
            act(lax.rem(mine + i, crs))
            return carry

        if crs == 2:
            act(1 - mine)
        else:
            lax.fori_loop(1, crs, one, 0)

    def greet(sub, core):
        pl.semaphore_signal(barrier, inc=1, device_id=(sub, core), device_id_type=MESH)

    each_sub(lambda sub: greet(sub, mine))
    each_crs(lambda core: greet(me, core))

    pairs = [
        (right_hbm, right_ref),
        (basis_hbm, basis_ref),
        (picked_hbm, picked_ref),
        (counts_hbm, counts_ref),
        (coarse_hbm, coarse_ref),
        (listed_hbm, listed_ref),
        (inverse_hbm, inverse_ref),
        (own_hbm, own_ref),
        (couple_hbm, couple_ref),
    ]
    loads = [
        pltpu.make_async_copy(there, here, load_sems.at[n])
        for n, (there, here) in enumerate(pairs)
    ]
    for load in loads:
        load.start()

    def swap_halves(block):
        return pltpu.roll(block, 4, 0)

    def stack_parts(block):
        width = block.shape[1]
        high = block.astype(LOW).astype(WIDE)
        low = block - high
        at_top = lax.broadcasted_iota(jnp.int32, (8, width), 0) < 4
        return jnp.where(at_top, high, pltpu.roll(low, 4, 0)).astype(LOW)

    def nt(a, b):
        return lax.dot_general(a, b, NT, preferred_element_type=WIDE)

    def nn(a, b):
        return jnp.dot(a, b, preferred_element_type=WIDE)

    def turn(source, target):
        for k in range(0, source.shape[1], LANES):
            target[k : k + LANES, :] = source[:, k : k + LANES].T

    def row_sum(a):
        return jnp.sum(a, axis=1, keepdims=True)

    def restrict(block):
        both = nt(stack_parts(block), basis_parts[...])
        both = both + pltpu.roll(both, LANES // 2, 1)
        both = jnp.where(lane_of < kc, both + swap_halves(both), 0.0)
        moved = both
        for t in range(1, together):
            moved = jnp.where(lax.rem(me, together) == t, pltpu.roll(both, t * kc, 1), moved)
        return moved

    def encode(value):
        high = value.astype(LOW).astype(WIDE)
        rest = value - high
        middle = rest.astype(LOW).astype(WIDE)
        low = rest - middle
        spread = jnp.where(lane_of == AT, high, 0.0)
        spread = jnp.where(lane_of == AT + 1, middle, spread)
        return jnp.where(lane_of == AT + 2, low, spread)

    def pack(block, extra):
        first = jnp.where(top, block[:, :LANES], swap_halves(block[:, LANES : 2 * LANES]))
        second = jnp.where(top, block[:, 2 * LANES :], swap_halves(extra))
        return jnp.concatenate([first, second], axis=0).astype(LOW)

    def send(number, tile):
        sent[number] = tile

        def one(sub):
            pltpu.make_async_remote_copy(
                src_ref=sent.at[number],
                dst_ref=held[number].at[me],
                send_sem=send_sem,
                recv_sem=recv_sems.at[number],
                device_id=(sub, mine),
                device_id_type=MESH,
            ).start()

        each_sub(one)

    def receive(number):
        arrived = held[number].at[pl.ds(0, subs - 1)]
        pltpu.make_async_copy(arrived, arrived, recv_sems.at[number]).wait()

    def send_share(number, block):
        share[number, mine] = block

        def one(core):
            pltpu.make_async_remote_copy(
                src_ref=share.at[number, mine],
                dst_ref=share.at[number, mine],
                send_sem=share_send_sem,
                recv_sem=share_sems.at[number],
                device_id=(me, core),
                device_id_type=MESH,
            ).start()

        each_crs(one)

    def receive_share(number):
        arrived = share.at[number, pl.ds(0, crs - 1)]
        pltpu.make_async_copy(arrived, arrived, share_sems.at[number]).wait()
        total = share[number, 0]
        for c in range(1, crs):
            total = total + share[number, c]
        return total

    def lines_of(number):
        lines = []
        for j in range(slots):
            tile = held[number][listed_ref[0, 0, j]].astype(WIDE)
            first = tile[:8]
            lines.append(jnp.concatenate([first, swap_halves(first), tile[8:]], axis=1))
        return lines

    def margin(number):
        fetched = nn(jnp.concatenate(lines_of(number), axis=0).astype(LOW), pick[...])
        parts = [
            fetched[8 * j : 8 * j + 8, LANES * j : LANES * j + LANES] for j in range(slots)
        ]
        return jnp.concatenate(parts, axis=1).astype(LOW)

    def couple(number):
        wide = jnp.concatenate(lines_of(number), axis=1).astype(LOW)
        return nn(wide, couple_wide[...])

    def group_sums(number):
        sums = []
        for g in range(groups):
            members = range(g * together, min(subs, (g + 1) * together))
            tiles = [held[number][s].astype(WIDE)[8:] for s in members]
            sums.append(functools.reduce(jnp.add, tiles))
        return sums

    def with_scalars(solved, totals):
        if share_lanes > LANES:
            totals = jnp.concatenate(
                [totals, jnp.zeros((8, share_lanes - LANES), WIDE)], axis=1
            )
        at_top = lax.broadcasted_iota(jnp.int32, (8, share_lanes), 0) < 4
        return jnp.where(at_top, pltpu.roll(solved, 4, 0), totals)

    def scalar(block):
        return row_sum(jnp.where((lane_of >= AT) & (lane_of < AT + 3), block, 0.0))

    def prolong(total):
        parts = stack_parts(total)
        both = nn(jnp.concatenate([parts, parts], axis=1), shifted_parts[...])
        return both + pltpu.roll(both, 4, 0)

    def precondition(number, share_number, own_part):
        receive(number)
        sums = group_sums(number)
        solved = nt(jnp.concatenate(sums, axis=1).astype(LOW), coarse_wide[...])
        totals = functools.reduce(jnp.add, sums)
        send_share(share_number, with_scalars(solved, totals))
        fine = own_part + nn(margin(number), inverse_t[rows:])
        total = receive_share(share_number)
        return fine + prolong(total), swap_halves(total[:, :LANES])

    loads[0].wait()
    loads[1].wait()
    right = jnp.concatenate(
        [right_ref[q] for q in range(cols)] + [jnp.zeros((8 - cols, rows), WIDE)], axis=0
    )
    basis = basis_ref[0, 0]
    basis_high = basis.astype(LOW).astype(WIDE)
    gap = jnp.zeros((LANES // 2 - kc, rows), WIDE)
    basis_parts[...] = jnp.concatenate(
        [basis_high, gap, basis - basis_high, gap], axis=0
    ).astype(LOW)
    extra = restrict(right) + encode(row_sum(right * right))
    tile = pack(right, extra)
    held_0[me] = tile
    pl.semaphore_wait(barrier, subs - 1 + crs - 1)
    send(0, tile)

    loads[2].wait()
    loads[3].wait()
    live = lax.broadcasted_iota(jnp.int32, (slots, LANES), 0) < counts_ref[0, 0, 0]
    wanted = jnp.where(
        live, jnp.concatenate([picked_ref[0, j] for j in range(slots)], axis=0), -1
    )
    row_index = lax.broadcasted_iota(jnp.int32, (rows, LANES), 0)
    for j in range(slots):
        pick[:, j * LANES : (j + 1) * LANES] = jnp.where(
            row_index == wanted[j : j + 1], 1.0, 0.0
        ).astype(LOW)
    shifted[...] = jnp.zeros_like(shifted)
    shifted[pl.ds(pl.multiple_of(mine * kc, 8), kc), :] = basis
    shifted_full = shifted[...]
    shifted_high = shifted_full.astype(LOW)
    shifted_parts[:share_lanes] = shifted_high
    shifted_parts[share_lanes:] = (shifted_full - shifted_high.astype(WIDE)).astype(LOW)
    loads[4].wait()
    coarse_rows = crs * kc
    coarse_cols = subs * kc
    coarse_wide[...] = jnp.zeros_like(coarse_wide)
    coarse_lane = lax.broadcasted_iota(jnp.int32, (coarse_rows, LANES), 1)
    for g in range(groups):
        first = g * together * kc
        count = min(together * kc, coarse_cols - first)
        base = first // LANES * LANES
        offset = first - base
        width = LANES if offset + count <= LANES else 2 * LANES
        window = coarse_ref[:, base : base + width].astype(WIDE)
        if offset:
            window = pltpu.roll(window, width - offset, 1)
        coarse_wide[:coarse_rows, g * LANES : (g + 1) * LANES] = jnp.where(
            coarse_lane < count, window[:, :LANES], 0.0
        ).astype(LOW)
    loads[5].wait()
    loads[6].wait()
    turn(inverse_ref, inverse_t)
    own_fine = nn(right.astype(LOW), inverse_t[:rows])

    first_z, totals = precondition(0, 0, own_fine)
    right_square = scalar(totals) / all_rows
    start = jnp.sqrt(right_square + EPSILON)
    start_square_scale = 1.0 / (all_rows * (right_square + EPSILON))

    nothing = jnp.zeros((8, LANES), WIDE)
    send(1, pack(first_z, nothing))
    loads[7].wait()
    loads[8].wait()
    turn(own_ref, own_t)
    for j in range(slots):
        block = slice(j * LANES, (j + 1) * LANES)
        couple_wide[j * rows : (j + 1) * rows, :] = nt(
            pick[:, block], couple_ref[:, block]
        ).astype(LOW)
    own_part = nn(first_z.astype(LOW), own_t[...])
    receive(1)
    mapped = own_part + couple(1)

    extra = restrict(mapped) + encode(row_sum(mapped * right))
    tile = pack(mapped, extra)
    held_2[me] = tile
    send(2, tile)
    own_fine = nn(mapped.astype(LOW), inverse_t[:rows])
    mapped_z, totals = precondition(2, 1, own_fine)
    height_11 = scalar(totals) * start_square_scale
    second_z = mapped_z - height_11 * first_z
    second = mapped - height_11 * right

    send(3, pack(second_z, nothing))
    own_part = nn(second_z.astype(LOW), own_t[...])
    products = [row_sum(second * second), row_sum(right * second)]
    receive(3)
    last = own_part + couple(3)

    products = products + [row_sum(last * right), row_sum(last * second), row_sum(last * last)]
    line = jnp.zeros((8, LANES), WIDE)
    for d, value in enumerate(products):
        line = jnp.where((lane_of == d * 4 + row_of) & top, value, line)
    here = me * crs + mine
    everyone = subs * crs
    last_rows[here] = jnp.sum(line, axis=0, keepdims=True)

    def send_last(sub, core):
        pltpu.make_async_remote_copy(
            src_ref=last_rows.at[here],
            dst_ref=last_rows.at[here],
            send_sem=last_send_sem,
            recv_sem=last_sem,
            device_id=(sub, core),
            device_id_type=MESH,
        ).start()

    def send_last_to(sub):
        send_last(sub, mine)
        each_crs(lambda core: send_last(sub, core))

    each_sub(send_last_to)
    each_crs(lambda core: send_last(me, core))
    arrived = last_rows.at[pl.ds(0, everyone - 1)]
    pltpu.make_async_copy(arrived, arrived, last_sem).wait()
    whole = jnp.broadcast_to(jnp.sum(last_rows[...], axis=0), (8, LANES)) / all_rows

    def final(d):
        return row_sum(jnp.where(lane_of == d * 4 + row_of, whole, 0.0))

    second_square = final(0)
    length_1 = jnp.sqrt(second_square / (start * start) + EPSILON)
    scale = 1.0 / (start * length_1)
    start_scale = 1.0 / start
    gram_11 = right_square * start_scale * start_scale
    gram_12 = final(1) * start_scale * scale
    gram_22 = second_square * scale * scale
    height_12 = final(2) * start_scale * scale
    height_22 = final(3) * scale * scale
    last_square = final(4) * scale * scale
    rest = (
        last_square
        - height_12 * height_12 * (2.0 - gram_11)
        - height_22 * height_22 * (2.0 - gram_22)
        + 2.0 * height_12 * height_22 * gram_12
    )
    length_2 = jnp.sqrt(jnp.maximum(rest, 0.0) + EPSILON)
    weights = least_squares(start, [[height_11, length_1], [height_12, height_22, length_2]])
    result = (weights[0] * start_scale) * first_z + (weights[1] * scale) * second_z
    following = (last * scale - (height_12 * start_scale) * right - (height_22 * scale) * second) / length_2
    for q in range(cols):
        both_ref[0, q] = result[q : q + 1]
        both_ref[1, q] = following[q : q + 1]

    for number in range(ROUNDS):
        gone = held[number].at[pl.ds(0, subs - 1)]
        pltpu.make_async_copy(gone, gone, send_sem).wait()
    for number in range(SHARES):
        gone = share.at[number, pl.ds(0, crs - 1)]
        pltpu.make_async_copy(gone, gone, share_send_sem).wait()
    pltpu.make_async_copy(arrived, arrived, last_send_sem).wait()


def body(
    right_side,
    own_block,
    coupling,
    local_inverse,
    coarse_basis,
    coarse_inverse,
    neighbours,
    margin_rows,
    block_counts,
):
    cols, rows = right_side.shape[0], right_side.shape[3]
    subs, crs = lax.axis_size("sub"), lax.axis_size("crs")
    kc = coarse_basis.shape[2]
    slots, block_rows = margin_rows.shape[2:]
    coarse_rows = crs * kc
    share_lanes = -(-coarse_rows // LANES) * LANES
    together = (LANES - 8) // kc
    groups = -(-subs // together)
    sizes = (subs, crs, cols, rows, kc, slots, share_lanes, together, groups)
    vmem = pl.BlockSpec(memory_space=pltpu.VMEM)
    stays = pl.BlockSpec(memory_space=pltpu.HBM)
    both = pl.pallas_call(
        functools.partial(kernel, sizes),
        out_shape=pltpu.VMEM((2, cols, 1, rows), WIDE),
        in_specs=[stays] * 9,
        out_specs=vmem,
        scratch_shapes=[
            pltpu.VMEM((cols, 1, rows), WIDE),
            pltpu.VMEM((rows, rows), LOW),
            pltpu.VMEM((rows, slots * block_rows), LOW),
            pltpu.VMEM((rows, rows + slots * block_rows), LOW),
            pltpu.VMEM((1, 1, kc, rows), WIDE),
            pltpu.VMEM((coarse_rows, subs * kc), LOW),
            pltpu.SMEM((1, 1, slots), jnp.int32),
            pltpu.VMEM((1, slots, 1, block_rows), jnp.int32),
            pltpu.SMEM((1, 1, 1), jnp.int32),
            pltpu.VMEM((ROUNDS, 16, LANES), LOW),
            *[pltpu.VMEM((subs, 16, LANES), LOW) for number in range(ROUNDS)],
            pltpu.VMEM((SHARES, crs, 8, share_lanes), WIDE),
            pltpu.VMEM((subs * crs, 1, LANES), WIDE),
            pltpu.VMEM((rows, rows), LOW),
            pltpu.VMEM((slots * rows, rows), LOW),
            pltpu.VMEM((rows + slots * block_rows, rows), LOW),
            pltpu.VMEM((rows, slots * block_rows), LOW),
            pltpu.VMEM((share_lanes, groups * LANES), LOW),
            pltpu.VMEM((LANES, rows), LOW),
            pltpu.VMEM((share_lanes, rows), WIDE),
            pltpu.VMEM((2 * share_lanes, rows), LOW),
            pltpu.SemaphoreType.DMA((9,)),
            pltpu.SemaphoreType.DMA,
            pltpu.SemaphoreType.DMA((ROUNDS,)),
            pltpu.SemaphoreType.DMA,
            pltpu.SemaphoreType.DMA((SHARES,)),
            pltpu.SemaphoreType.DMA,
            pltpu.SemaphoreType.DMA,
        ],
        compiler_params=pltpu.CompilerParams(
            collective_id=0, has_side_effects=True, vmem_limit_bytes=63 * 1024 * 1024
        ),
    )(
        right_side.reshape(cols, 1, rows),
        own_block.reshape(rows, -1),
        coupling.reshape(rows, -1),
        local_inverse.reshape(rows, -1),
        coarse_basis,
        coarse_inverse.reshape(coarse_rows, -1),
        neighbours,
        margin_rows.reshape(1, slots, 1, block_rows),
        block_counts.reshape(1, 1, 1),
    )
    shape = (cols, 1, 1, rows)
    return both[0].reshape(shape), both[1].reshape(shape)


def solution(mesh):
    in_specs = (
        P(None, "sub", "crs", None),
        P("sub", "crs", None, None),
        P("sub", "crs", None, None),
        P("sub", "crs", None, None),
        P("sub", "crs", None, None),
        P("sub", None, "crs", None),
        P("sub", "crs", None),
        P("sub", "crs", None, None),
        P("sub", "crs"),
    )
    out_specs = (P(None, "sub", "crs", None), P(None, "sub", "crs", None))
    return jax.shard_map(body, mesh=mesh, in_specs=in_specs, out_specs=out_specs, check_vma=False)
```

```python
import functools

import jax
import jax.numpy as jnp
from jax import lax
from jax.experimental import pallas as pl
from jax.experimental.pallas import tpu as pltpu
from jax.sharding import PartitionSpec as P

EPSILON = 1e-06
MESH = pl.DeviceIdType.MESH
LANES = 128
ROUNDS = 4
SHARES = 2
ORDER = (15, 11, 14, 13, 10, 9, 12, 8, 7, 6, 5, 4, 3, 2, 1)
AT = 120
NT = (((1,), (1,)), ((), ()))
LOW = jnp.bfloat16
WIDE = jnp.float32


def least_squares(start_norm, columns):
    cosines = []
    sine_terms = []
    triangle = []
    target = [start_norm] + [jnp.zeros_like(start_norm) for j in range(len(columns))]
    for j, column in enumerate(columns):
        column = list(column)
        for i in range(j):
            upper_value = cosines[i] * column[i] + sine_terms[i] * column[i + 1]
            column[i + 1] = -sine_terms[i] * column[i] + cosines[i] * column[i + 1]
            column[i] = upper_value
        radius = jnp.sqrt(column[j] * column[j] + column[j + 1] * column[j + 1])
        cosine = column[j] / radius
        sine_part = column[j + 1] / radius
        column[j] = radius
        target[j + 1] = -sine_part * target[j]
        target[j] = cosine * target[j]
        cosines.append(cosine)
        sine_terms.append(sine_part)
        triangle.append(column[: j + 1])
    weights = [None] * len(columns)
    for j in reversed(range(len(columns))):
        running = target[j]
        for k in range(j + 1, len(columns)):
            running = running - triangle[k][j] * weights[k]
        weights[j] = running / triangle[j][j]
    return weights


def kernel(
    sizes,
    right_hbm,
    own_hbm,
    couple_hbm,
    inverse_hbm,
    basis_hbm,
    coarse_hbm,
    listed_hbm,
    picked_hbm,
    counts_hbm,
    both_ref,
    right_ref,
    own_ref,
    couple_ref,
    inverse_ref,
    basis_ref,
    coarse_ref,
    listed_ref,
    picked_ref,
    counts_ref,
    sent,
    held_0,
    held_1,
    held_2,
    held_3,
    share,
    last_rows,
    own_t,
    couple_t,
    inverse_t,
    pick,
    coarse_wide,
    basis_parts,
    shifted,
    shifted_parts,
    load_sems,
    send_sem,
    recv_sems,
    share_send_sem,
    share_sems,
    last_send_sem,
    last_sem,
):
    subs, crs, cols, rows, kc, slots, share_lanes, together, groups = sizes
    held = (held_0, held_1, held_2, held_3)
    me = lax.axis_index("sub")
    mine = lax.axis_index("crs")
    all_rows = float(rows * subs * crs)
    row_of = lax.broadcasted_iota(jnp.int32, (8, LANES), 0)
    lane_of = lax.broadcasted_iota(jnp.int32, (8, LANES), 1)
    top = row_of < 4

    pairs = [
        (right_hbm, right_ref),
        (basis_hbm, basis_ref),
        (picked_hbm, picked_ref),
        (counts_hbm, counts_ref),
        (coarse_hbm, coarse_ref),
        (listed_hbm, listed_ref),
        (inverse_hbm, inverse_ref),
        (own_hbm, own_ref),
        (couple_hbm, couple_ref),
    ]
    loads = [
        pltpu.make_async_copy(there, here, load_sems.at[n])
        for n, (there, here) in enumerate(pairs)
    ]
    loads[0].start()
    loads[1].start()
    barrier = pltpu.get_barrier_semaphore()

    short = subs & (subs - 1) == 0 and subs <= 16

    def flipped(index, mask, bits):
        moved = index
        for k in range(bits):
            if mask >> k & 1:
                moved = moved + (1 << k) - (index // (1 << k)) % 2 * (2 << k)
        return moved

    def each_sub(act):
        if short:
            for mask in ORDER:
                if mask < subs:
                    act(flipped(me, mask, 4))
        else:

            def one(i, carry):
                act(lax.rem(me + i, subs))
                return carry

            lax.fori_loop(1, subs, one, 0)

    def each_crs(act):
        def one(i, carry):
            act(lax.rem(mine + i, crs))
            return carry

        if crs == 2:
            act(1 - mine)
        else:
            lax.fori_loop(1, crs, one, 0)

    def greet(sub, core):
        pl.semaphore_signal(barrier, inc=1, device_id=(sub, core), device_id_type=MESH)

    each_sub(lambda sub: greet(sub, mine))
    each_crs(lambda core: greet(me, core))

    for load in loads[2:]:
        load.start()

    def swap_halves(block):
        return pltpu.roll(block, 4, 0)

    def stack_parts(block):
        width = block.shape[1]
        high = block.astype(LOW).astype(WIDE)
        low = block - high
        at_top = lax.broadcasted_iota(jnp.int32, (8, width), 0) < 4
        return jnp.where(at_top, high, pltpu.roll(low, 4, 0)).astype(LOW)

    def nt(a, b):
        return lax.dot_general(a, b, NT, preferred_element_type=WIDE)

    def nn(a, b):
        return jnp.dot(a, b, preferred_element_type=WIDE)

    def turn(source, target):
        for k in range(0, source.shape[1], LANES):
            target[k : k + LANES, :] = source[:, k : k + LANES].T

    def row_sum(a):
        return jnp.sum(a, axis=1, keepdims=True)

    def restrict(block):
        both = nt(stack_parts(block), basis_parts[...])
        both = both + pltpu.roll(both, LANES // 2, 1)
        both = jnp.where(lane_of < kc, both + swap_halves(both), 0.0)
        moved = both
        for t in range(1, together):
            moved = jnp.where(lax.rem(me, together) == t, pltpu.roll(both, t * kc, 1), moved)
        return moved

    def encode(value):
        high = value.astype(LOW).astype(WIDE)
        rest = value - high
        middle = rest.astype(LOW).astype(WIDE)
        low = rest - middle
        spread = jnp.where(lane_of == AT, high, 0.0)
        spread = jnp.where(lane_of == AT + 1, middle, spread)
        return jnp.where(lane_of == AT + 2, low, spread)

    def pack(block, extra):
        first = jnp.where(top, block[:, :LANES], swap_halves(block[:, LANES : 2 * LANES]))
        second = jnp.where(top, block[:, 2 * LANES :], swap_halves(extra))
        return jnp.concatenate([first, second], axis=0).astype(LOW)

    def send(number, tile):
        sent[number] = tile

        def one(sub):
            pltpu.make_async_remote_copy(
                src_ref=sent.at[number],
                dst_ref=held[number].at[me],
                send_sem=send_sem,
                recv_sem=recv_sems.at[number],
                device_id=(sub, mine),
                device_id_type=MESH,
            ).start()

        each_sub(one)

    def receive(number):
        arrived = held[number].at[pl.ds(0, subs - 1)]
        pltpu.make_async_copy(arrived, arrived, recv_sems.at[number]).wait()

    def send_share(number, block):
        share[number, mine] = block

        def one(core):
            pltpu.make_async_remote_copy(
                src_ref=share.at[number, mine],
                dst_ref=share.at[number, mine],
                send_sem=share_send_sem,
                recv_sem=share_sems.at[number],
                device_id=(me, core),
                device_id_type=MESH,
            ).start()

        each_crs(one)

    def receive_share(number):
        arrived = share.at[number, pl.ds(0, crs - 1)]
        pltpu.make_async_copy(arrived, arrived, share_sems.at[number]).wait()
        total = share[number, 0]
        for c in range(1, crs):
            total = total + share[number, c]
        return total

    def fetch(number):
        lines = []
        for j in range(slots):
            tile = held[number][listed_ref[0, 0, j]].astype(WIDE)
            first = tile[:8]
            lines.append(jnp.concatenate([first, swap_halves(first), tile[8:]], axis=1))
        return nn(jnp.concatenate(lines, axis=0).astype(LOW), pick[...])

    def margin(fetched):
        parts = [
            fetched[8 * j : 8 * j + 8, LANES * j : LANES * j + LANES] for j in range(slots)
        ]
        return jnp.concatenate(parts, axis=1).astype(LOW)

    def group_sums(number):
        sums = []
        for g in range(groups):
            members = range(g * together, min(subs, (g + 1) * together))
            tiles = [held[number][s].astype(WIDE)[8:] for s in members]
            sums.append(functools.reduce(jnp.add, tiles))
        return sums

    def with_scalars(solved, totals):
        if share_lanes > LANES:
            totals = jnp.concatenate(
                [totals, jnp.zeros((8, share_lanes - LANES), WIDE)], axis=1
            )
        at_top = lax.broadcasted_iota(jnp.int32, (8, share_lanes), 0) < 4
        return jnp.where(at_top, pltpu.roll(solved, 4, 0), totals)

    def scalar(block):
        return row_sum(jnp.where((lane_of >= AT) & (lane_of < AT + 3), block, 0.0))

    def prolong(total):
        parts = stack_parts(total)
        both = nn(jnp.concatenate([parts, parts], axis=1), shifted_parts[...])
        return both + pltpu.roll(both, 4, 0)

    def precondition(number, share_number, own_part):
        receive(number)
        sums = group_sums(number)
        solved = nt(jnp.concatenate(sums, axis=1).astype(LOW), coarse_wide[...])
        totals = functools.reduce(jnp.add, sums)
        send_share(share_number, with_scalars(solved, totals))
        fine = own_part + nn(margin(fetch(number)), inverse_t[rows:])
        total = receive_share(share_number)
        return fine + prolong(total), swap_halves(total[:, :LANES])

    loads[0].wait()
    loads[1].wait()
    right = jnp.concatenate(
        [right_ref[q] for q in range(cols)] + [jnp.zeros((8 - cols, rows), WIDE)], axis=0
    )
    basis = basis_ref[0, 0]
    basis_high = basis.astype(LOW).astype(WIDE)
    gap = jnp.zeros((LANES // 2 - kc, rows), WIDE)
    basis_parts[...] = jnp.concatenate(
        [basis_high, gap, basis - basis_high, gap], axis=0
    ).astype(LOW)
    extra = restrict(right) + encode(row_sum(right * right))
    tile = pack(right, extra)
    held_0[me] = tile
    pl.semaphore_wait(barrier, subs - 1 + crs - 1)
    send(0, tile)

    loads[2].wait()
    loads[3].wait()
    live = lax.broadcasted_iota(jnp.int32, (slots, LANES), 0) < counts_ref[0, 0, 0]
    wanted = jnp.where(
        live, jnp.concatenate([picked_ref[0, j] for j in range(slots)], axis=0), -1
    )
    row_index = lax.broadcasted_iota(jnp.int32, (rows, LANES), 0)
    for j in range(slots):
        pick[:, j * LANES : (j + 1) * LANES] = jnp.where(
            row_index == wanted[j : j + 1], 1.0, 0.0
        ).astype(LOW)
    shifted[...] = jnp.zeros_like(shifted)
    shifted[pl.ds(pl.multiple_of(mine * kc, 8), kc), :] = basis
    shifted_full = shifted[...]
    shifted_high = shifted_full.astype(LOW)
    shifted_parts[:share_lanes] = shifted_high
    shifted_parts[share_lanes:] = (shifted_full - shifted_high.astype(WIDE)).astype(LOW)
    loads[4].wait()
    coarse_rows = crs * kc
    coarse_cols = subs * kc
    coarse_wide[...] = jnp.zeros_like(coarse_wide)
    coarse_lane = lax.broadcasted_iota(jnp.int32, (coarse_rows, LANES), 1)
    for g in range(groups):
        first = g * together * kc
        count = min(together * kc, coarse_cols - first)
        base = first // LANES * LANES
        offset = first - base
        width = LANES if offset + count <= LANES else 2 * LANES
        window = coarse_ref[:, base : base + width].astype(WIDE)
        if offset:
            window = pltpu.roll(window, width - offset, 1)
        coarse_wide[:coarse_rows, g * LANES : (g + 1) * LANES] = jnp.where(
            coarse_lane < count, window[:, :LANES], 0.0
        ).astype(LOW)
    loads[5].wait()
    loads[6].wait()
    turn(inverse_ref, inverse_t)
    own_fine = nn(right.astype(LOW), inverse_t[:rows])

    first_z, totals = precondition(0, 0, own_fine)
    right_square = scalar(totals) / all_rows
    start = jnp.sqrt(right_square + EPSILON)
    start_square_scale = 1.0 / (all_rows * (right_square + EPSILON))

    nothing = jnp.zeros((8, LANES), WIDE)
    send(1, pack(first_z, nothing))
    loads[7].wait()
    loads[8].wait()
    turn(own_ref, own_t)
    turn(couple_ref, couple_t)
    own_part = nn(first_z.astype(LOW), own_t[...])
    receive(1)
    mapped = own_part + nn(margin(fetch(1)), couple_t[...])

    extra = restrict(mapped) + encode(row_sum(mapped * right))
    tile = pack(mapped, extra)
    held_2[me] = tile
    send(2, tile)
    own_fine = nn(mapped.astype(LOW), inverse_t[:rows])
    mapped_z, totals = precondition(2, 1, own_fine)
    height_11 = scalar(totals) * start_square_scale
    second_z = mapped_z - height_11 * first_z
    second = mapped - height_11 * right

    send(3, pack(second_z, nothing))
    own_part = nn(second_z.astype(LOW), own_t[...])
    products = [row_sum(second * second), row_sum(right * second)]
    receive(3)
    last = own_part + nn(margin(fetch(3)), couple_t[...])

    products = products + [row_sum(last * right), row_sum(last * second), row_sum(last * last)]
    line = jnp.zeros((8, LANES), WIDE)
    for d, value in enumerate(products):
        line = jnp.where((lane_of == d * 4 + row_of) & top, value, line)
    here = me * crs + mine
    everyone = subs * crs
    last_rows[here] = jnp.sum(line, axis=0, keepdims=True)

    def send_last(sub, core):
        pltpu.make_async_remote_copy(
            src_ref=last_rows.at[here],
            dst_ref=last_rows.at[here],
            send_sem=last_send_sem,
            recv_sem=last_sem,
            device_id=(sub, core),
            device_id_type=MESH,
        ).start()

    def send_last_to(sub):
        send_last(sub, mine)
        each_crs(lambda core: send_last(sub, core))

    each_sub(send_last_to)
    each_crs(lambda core: send_last(me, core))
    arrived = last_rows.at[pl.ds(0, everyone - 1)]
    pltpu.make_async_copy(arrived, arrived, last_sem).wait()
    whole = jnp.broadcast_to(jnp.sum(last_rows[...], axis=0), (8, LANES)) / all_rows

    def final(d):
        return row_sum(jnp.where(lane_of == d * 4 + row_of, whole, 0.0))

    second_square = final(0)
    length_1 = jnp.sqrt(second_square / (start * start) + EPSILON)
    scale = 1.0 / (start * length_1)
    start_scale = 1.0 / start
    gram_11 = right_square * start_scale * start_scale
    gram_12 = final(1) * start_scale * scale
    gram_22 = second_square * scale * scale
    height_12 = final(2) * start_scale * scale
    height_22 = final(3) * scale * scale
    last_square = final(4) * scale * scale
    rest = (
        last_square
        - height_12 * height_12 * (2.0 - gram_11)
        - height_22 * height_22 * (2.0 - gram_22)
        + 2.0 * height_12 * height_22 * gram_12
    )
    length_2 = jnp.sqrt(jnp.maximum(rest, 0.0) + EPSILON)
    weights = least_squares(start, [[height_11, length_1], [height_12, height_22, length_2]])
    result = (weights[0] * start_scale) * first_z + (weights[1] * scale) * second_z
    following = (last * scale - (height_12 * start_scale) * right - (height_22 * scale) * second) / length_2
    for q in range(cols):
        both_ref[0, q] = result[q : q + 1]
        both_ref[1, q] = following[q : q + 1]

    for number in range(ROUNDS):
        gone = held[number].at[pl.ds(0, subs - 1)]
        pltpu.make_async_copy(gone, gone, send_sem).wait()
    for number in range(SHARES):
        gone = share.at[number, pl.ds(0, crs - 1)]
        pltpu.make_async_copy(gone, gone, share_send_sem).wait()
    pltpu.make_async_copy(arrived, arrived, last_send_sem).wait()


def body(
    right_side,
    own_block,
    coupling,
    local_inverse,
    coarse_basis,
    coarse_inverse,
    neighbours,
    margin_rows,
    block_counts,
):
    cols, rows = right_side.shape[0], right_side.shape[3]
    subs, crs = lax.axis_size("sub"), lax.axis_size("crs")
    kc = coarse_basis.shape[2]
    slots, block_rows = margin_rows.shape[2:]
    coarse_rows = crs * kc
    share_lanes = -(-coarse_rows // LANES) * LANES
    together = (LANES - 8) // kc
    groups = -(-subs // together)
    sizes = (subs, crs, cols, rows, kc, slots, share_lanes, together, groups)
    vmem = pl.BlockSpec(memory_space=pltpu.VMEM)
    stays = pl.BlockSpec(memory_space=pltpu.HBM)
    both = pl.pallas_call(
        functools.partial(kernel, sizes),
        out_shape=pltpu.VMEM((2, cols, 1, rows), WIDE),
        in_specs=[stays] * 9,
        out_specs=vmem,
        scratch_shapes=[
            pltpu.VMEM((cols, 1, rows), WIDE),
            pltpu.VMEM((rows, rows), LOW),
            pltpu.VMEM((rows, slots * block_rows), LOW),
            pltpu.VMEM((rows, rows + slots * block_rows), LOW),
            pltpu.VMEM((1, 1, kc, rows), WIDE),
            pltpu.VMEM((coarse_rows, subs * kc), LOW),
            pltpu.SMEM((1, 1, slots), jnp.int32),
            pltpu.VMEM((1, slots, 1, block_rows), jnp.int32),
            pltpu.SMEM((1, 1, 1), jnp.int32),
            pltpu.VMEM((ROUNDS, 16, LANES), LOW),
            *[pltpu.VMEM((subs, 16, LANES), LOW) for number in range(ROUNDS)],
            pltpu.VMEM((SHARES, crs, 8, share_lanes), WIDE),
            pltpu.VMEM((subs * crs, 1, LANES), WIDE),
            pltpu.VMEM((rows, rows), LOW),
            pltpu.VMEM((slots * block_rows, rows), LOW),
            pltpu.VMEM((rows + slots * block_rows, rows), LOW),
            pltpu.VMEM((rows, slots * block_rows), LOW),
            pltpu.VMEM((share_lanes, groups * LANES), LOW),
            pltpu.VMEM((LANES, rows), LOW),
            pltpu.VMEM((share_lanes, rows), WIDE),
            pltpu.VMEM((2 * share_lanes, rows), LOW),
            pltpu.SemaphoreType.DMA((9,)),
            pltpu.SemaphoreType.DMA,
            pltpu.SemaphoreType.DMA((ROUNDS,)),
            pltpu.SemaphoreType.DMA,
            pltpu.SemaphoreType.DMA((SHARES,)),
            pltpu.SemaphoreType.DMA,
            pltpu.SemaphoreType.DMA,
        ],
        compiler_params=pltpu.CompilerParams(
            collective_id=0, has_side_effects=True, vmem_limit_bytes=63 * 1024 * 1024
        ),
    )(
        right_side.reshape(cols, 1, rows),
        own_block.reshape(rows, -1),
        coupling.reshape(rows, -1),
        local_inverse.reshape(rows, -1),
        coarse_basis,
        coarse_inverse.reshape(coarse_rows, -1),
        neighbours,
        margin_rows.reshape(1, slots, 1, block_rows),
        block_counts.reshape(1, 1, 1),
    )
    shape = (cols, 1, 1, rows)
    return both[0].reshape(shape), both[1].reshape(shape)


def solution(mesh):
    in_specs = (
        P(None, "sub", "crs", None),
        P("sub", "crs", None, None),
        P("sub", "crs", None, None),
        P("sub", "crs", None, None),
        P("sub", "crs", None, None),
        P("sub", None, "crs", None),
        P("sub", "crs", None),
        P("sub", "crs", None, None),
        P("sub", "crs"),
    )
    out_specs = (P(None, "sub", "crs", None), P(None, "sub", "crs", None))
    return jax.shard_map(body, mesh=mesh, in_specs=in_specs, out_specs=out_specs, check_vma=False)
```

```python
import functools

import jax
import jax.numpy as jnp
from jax import lax
from jax.experimental import pallas as pl
from jax.experimental.pallas import tpu as pltpu
from jax.sharding import PartitionSpec as P

EPSILON = 1e-06
MESH = pl.DeviceIdType.MESH
LANES = 128
ROUNDS = 4
SHARES = 2
ORDER = (15, 11, 14, 13, 10, 9, 12, 8, 7, 6, 5, 4, 3, 2, 1)
AT = 120
NT = (((1,), (1,)), ((), ()))
LOW = jnp.bfloat16
WIDE = jnp.float32


def least_squares(start_norm, columns):
    cosines = []
    sine_terms = []
    triangle = []
    target = [start_norm] + [jnp.zeros_like(start_norm) for j in range(len(columns))]
    for j, column in enumerate(columns):
        column = list(column)
        for i in range(j):
            upper_value = cosines[i] * column[i] + sine_terms[i] * column[i + 1]
            column[i + 1] = -sine_terms[i] * column[i] + cosines[i] * column[i + 1]
            column[i] = upper_value
        radius = jnp.sqrt(column[j] * column[j] + column[j + 1] * column[j + 1])
        cosine = column[j] / radius
        sine_part = column[j + 1] / radius
        column[j] = radius
        target[j + 1] = -sine_part * target[j]
        target[j] = cosine * target[j]
        cosines.append(cosine)
        sine_terms.append(sine_part)
        triangle.append(column[: j + 1])
    weights = [None] * len(columns)
    for j in reversed(range(len(columns))):
        running = target[j]
        for k in range(j + 1, len(columns)):
            running = running - triangle[k][j] * weights[k]
        weights[j] = running / triangle[j][j]
    return weights


def kernel(
    sizes,
    right_hbm,
    own_hbm,
    couple_hbm,
    inverse_hbm,
    basis_hbm,
    coarse_hbm,
    listed_hbm,
    picked_hbm,
    counts_hbm,
    both_ref,
    right_ref,
    own_ref,
    couple_ref,
    inverse_ref,
    basis_ref,
    coarse_ref,
    listed_ref,
    picked_ref,
    counts_ref,
    sent,
    held_0,
    held_1,
    held_2,
    held_3,
    share,
    last_rows,
    own_t,
    couple_t,
    inverse_t,
    pick,
    coarse_wide,
    basis_parts,
    shifted,
    shifted_parts,
    load_sems,
    send_sem,
    recv_sems,
    share_send_sem,
    share_sems,
    last_send_sem,
    last_sem,
):
    subs, crs, cols, rows, kc, slots, share_lanes, together, groups = sizes
    held = (held_0, held_1, held_2, held_3)
    me = lax.axis_index("sub")
    mine = lax.axis_index("crs")
    all_rows = float(rows * subs * crs)
    row_of = lax.broadcasted_iota(jnp.int32, (8, LANES), 0)
    lane_of = lax.broadcasted_iota(jnp.int32, (8, LANES), 1)
    top = row_of < 4

    barrier = pltpu.get_barrier_semaphore()

    short = subs & (subs - 1) == 0 and subs <= 16

    def flipped(index, mask, bits):
        moved = index
        for k in range(bits):
            if mask >> k & 1:
                moved = moved + (1 << k) - (index // (1 << k)) % 2 * (2 << k)
        return moved

    def each_sub(act):
        if short:
            for mask in ORDER:
                if mask < subs:
                    act(flipped(me, mask, 4))
        else:

            def one(i, carry):
                act(lax.rem(me + i, subs))
                return carry

            lax.fori_loop(1, subs, one, 0)

    def each_crs(act):
        def one(i, carry):
            act(lax.rem(mine + i, crs))
            return carry

        if crs == 2:
            act(1 - mine)
        else:
            lax.fori_loop(1, crs, one, 0)

    def greet(sub, core):
        pl.semaphore_signal(barrier, inc=1, device_id=(sub, core), device_id_type=MESH)

    each_sub(lambda sub: greet(sub, mine))
    each_crs(lambda core: greet(me, core))

    pairs = [
        (right_hbm, right_ref),
        (basis_hbm, basis_ref),
        (picked_hbm, picked_ref),
        (counts_hbm, counts_ref),
        (coarse_hbm, coarse_ref),
        (listed_hbm, listed_ref),
        (inverse_hbm, inverse_ref),
        (own_hbm, own_ref),
        (couple_hbm, couple_ref),
    ]
    loads = [
        pltpu.make_async_copy(there, here, load_sems.at[n])
        for n, (there, here) in enumerate(pairs)
    ]
    for load in loads:
        load.start()

    def swap_halves(block):
        return pltpu.roll(block, 4, 0)

    def stack_parts(block):
        width = block.shape[1]
        high = block.astype(LOW).astype(WIDE)
        low = block - high
        at_top = lax.broadcasted_iota(jnp.int32, (8, width), 0) < 4
        return jnp.where(at_top, high, pltpu.roll(low, 4, 0)).astype(LOW)

    def nt(a, b):
        return lax.dot_general(a, b, NT, preferred_element_type=WIDE)

    def nn(a, b):
        return jnp.dot(a, b, preferred_element_type=WIDE)

    def turn(source, target):
        for k in range(0, source.shape[1], LANES):
            target[k : k + LANES, :] = source[:, k : k + LANES].T

    def row_sum(a):
        return jnp.sum(a, axis=1, keepdims=True)

    def restrict(block):
        both = nt(stack_parts(block), basis_parts[...])
        both = both + pltpu.roll(both, LANES // 2, 1)
        both = jnp.where(lane_of < kc, both + swap_halves(both), 0.0)
        moved = both
        for t in range(1, together):
            moved = jnp.where(lax.rem(me, together) == t, pltpu.roll(both, t * kc, 1), moved)
        return moved

    def encode(value):
        high = value.astype(LOW).astype(WIDE)
        rest = value - high
        middle = rest.astype(LOW).astype(WIDE)
        low = rest - middle
        spread = jnp.where(lane_of == AT, high, 0.0)
        spread = jnp.where(lane_of == AT + 1, middle, spread)
        return jnp.where(lane_of == AT + 2, low, spread)

    def pack(block, extra):
        first = jnp.where(top, block[:, :LANES], swap_halves(block[:, LANES : 2 * LANES]))
        second = jnp.where(top, block[:, 2 * LANES :], swap_halves(extra))
        return jnp.concatenate([first, second], axis=0).astype(LOW)

    def send(number, tile):
        sent[number] = tile

        def one(sub):
            pltpu.make_async_remote_copy(
                src_ref=sent.at[number],
                dst_ref=held[number].at[me],
                send_sem=send_sem,
                recv_sem=recv_sems.at[number],
                device_id=(sub, mine),
                device_id_type=MESH,
            ).start()

        each_sub(one)

    def receive(number):
        arrived = held[number].at[pl.ds(0, subs - 1)]
        pltpu.make_async_copy(arrived, arrived, recv_sems.at[number]).wait()

    def send_share(number, block):
        share[number, mine] = block

        def one(core):
            pltpu.make_async_remote_copy(
                src_ref=share.at[number, mine],
                dst_ref=share.at[number, mine],
                send_sem=share_send_sem,
                recv_sem=share_sems.at[number],
                device_id=(me, core),
                device_id_type=MESH,
            ).start()

        each_crs(one)

    def receive_share(number):
        arrived = share.at[number, pl.ds(0, crs - 1)]
        pltpu.make_async_copy(arrived, arrived, share_sems.at[number]).wait()
        total = share[number, 0]
        for c in range(1, crs):
            total = total + share[number, c]
        return total

    def fetch(number):
        lines = []
        for j in range(slots):
            tile = held[number][listed_ref[0, 0, j]].astype(WIDE)
            first = tile[:8]
            lines.append(jnp.concatenate([first, swap_halves(first), tile[8:]], axis=1))
        return nn(jnp.concatenate(lines, axis=0).astype(LOW), pick[...])

    def margin(fetched):
        parts = [
            fetched[8 * j : 8 * j + 8, LANES * j : LANES * j + LANES] for j in range(slots)
        ]
        return jnp.concatenate(parts, axis=1).astype(LOW)

    def group_sums(number):
        sums = []
        for g in range(groups):
            members = range(g * together, min(subs, (g + 1) * together))
            tiles = [held[number][s].astype(WIDE)[8:] for s in members]
            sums.append(functools.reduce(jnp.add, tiles))
        return sums

    def with_scalars(solved, totals):
        if share_lanes > LANES:
            totals = jnp.concatenate(
                [totals, jnp.zeros((8, share_lanes - LANES), WIDE)], axis=1
            )
        at_top = lax.broadcasted_iota(jnp.int32, (8, share_lanes), 0) < 4
        return jnp.where(at_top, pltpu.roll(solved, 4, 0), totals)

    def scalar(block):
        return row_sum(jnp.where((lane_of >= AT) & (lane_of < AT + 3), block, 0.0))

    def prolong(total):
        parts = stack_parts(total)
        both = nn(jnp.concatenate([parts, parts], axis=1), shifted_parts[...])
        return both + pltpu.roll(both, 4, 0)

    def precondition(number, share_number, own_part):
        receive(number)
        sums = group_sums(number)
        solved = nt(jnp.concatenate(sums, axis=1).astype(LOW), coarse_wide[...])
        fetched = fetch(number)
        totals = functools.reduce(jnp.add, sums)
        send_share(share_number, with_scalars(solved, totals))
        if number:
            fine = own_part + nn(margin(fetched), inverse_t[rows:])
        else:
            fine = own_part + nt(margin(fetched), inverse_ref[:, rows:])
        total = receive_share(share_number)
        return fine + prolong(total), swap_halves(total[:, :LANES])

    loads[0].wait()
    loads[1].wait()
    right = jnp.concatenate(
        [right_ref[q] for q in range(cols)] + [jnp.zeros((8 - cols, rows), WIDE)], axis=0
    )
    basis = basis_ref[0, 0]
    basis_high = basis.astype(LOW).astype(WIDE)
    gap = jnp.zeros((LANES // 2 - kc, rows), WIDE)
    basis_parts[...] = jnp.concatenate(
        [basis_high, gap, basis - basis_high, gap], axis=0
    ).astype(LOW)
    extra = restrict(right) + encode(row_sum(right * right))
    tile = pack(right, extra)
    held_0[me] = tile
    pl.semaphore_wait(barrier, subs - 1 + crs - 1)
    send(0, tile)

    loads[2].wait()
    loads[3].wait()
    live = lax.broadcasted_iota(jnp.int32, (slots, LANES), 0) < counts_ref[0, 0, 0]
    wanted = jnp.where(
        live, jnp.concatenate([picked_ref[0, j] for j in range(slots)], axis=0), -1
    )
    row_index = lax.broadcasted_iota(jnp.int32, (rows, LANES), 0)
    for j in range(slots):
        pick[:, j * LANES : (j + 1) * LANES] = jnp.where(
            row_index == wanted[j : j + 1], 1.0, 0.0
        ).astype(LOW)
    shifted[...] = jnp.zeros_like(shifted)
    shifted[pl.ds(pl.multiple_of(mine * kc, 8), kc), :] = basis
    shifted_full = shifted[...]
    shifted_high = shifted_full.astype(LOW)
    shifted_parts[:share_lanes] = shifted_high
    shifted_parts[share_lanes:] = (shifted_full - shifted_high.astype(WIDE)).astype(LOW)
    loads[4].wait()
    coarse_rows = crs * kc
    coarse_cols = subs * kc
    coarse_wide[...] = jnp.zeros_like(coarse_wide)
    coarse_lane = lax.broadcasted_iota(jnp.int32, (coarse_rows, LANES), 1)
    for g in range(groups):
        first = g * together * kc
        count = min(together * kc, coarse_cols - first)
        base = first // LANES * LANES
        offset = first - base
        width = LANES if offset + count <= LANES else 2 * LANES
        window = coarse_ref[:, base : base + width].astype(WIDE)
        if offset:
            window = pltpu.roll(window, width - offset, 1)
        coarse_wide[:coarse_rows, g * LANES : (g + 1) * LANES] = jnp.where(
            coarse_lane < count, window[:, :LANES], 0.0
        ).astype(LOW)
    loads[5].wait()
    loads[6].wait()
    own_fine = nt(right.astype(LOW), inverse_ref[:, :rows])

    first_z, totals = precondition(0, 0, own_fine)
    right_square = scalar(totals) / all_rows
    start = jnp.sqrt(right_square + EPSILON)

    nothing = jnp.zeros((8, LANES), WIDE)
    send(1, pack(first_z, nothing))
    loads[7].wait()
    loads[8].wait()
    turn(own_ref, own_t)
    turn(couple_ref, couple_t)
    own_part = nn(first_z.astype(LOW), own_t[...])
    receive(1)
    mapped = own_part + nn(margin(fetch(1)), couple_t[...])

    extra = restrict(mapped) + encode(row_sum(mapped * right))
    tile = pack(mapped, extra)
    held_2[me] = tile
    send(2, tile)
    turn(inverse_ref, inverse_t)
    own_fine = nn(mapped.astype(LOW), inverse_t[:rows])
    mapped_z, totals = precondition(2, 1, own_fine)
    height_11 = scalar(totals) / all_rows / (start * start)
    second_z = mapped_z - height_11 * first_z
    second = mapped - height_11 * right

    send(3, pack(second_z, nothing))
    own_part = nn(second_z.astype(LOW), own_t[...])
    products = [row_sum(second * second), row_sum(right * second)]
    receive(3)
    last = own_part + nn(margin(fetch(3)), couple_t[...])

    products = products + [row_sum(last * right), row_sum(last * second), row_sum(last * last)]
    line = jnp.zeros((8, LANES), WIDE)
    for d, value in enumerate(products):
        line = jnp.where((lane_of == d * 4 + row_of) & top, value, line)
    here = me * crs + mine
    everyone = subs * crs
    last_rows[here] = jnp.sum(line, axis=0, keepdims=True)

    def send_last(sub, core):
        pltpu.make_async_remote_copy(
            src_ref=last_rows.at[here],
            dst_ref=last_rows.at[here],
            send_sem=last_send_sem,
            recv_sem=last_sem,
            device_id=(sub, core),
            device_id_type=MESH,
        ).start()

    def send_last_to(sub):
        send_last(sub, mine)
        each_crs(lambda core: send_last(sub, core))

    each_sub(send_last_to)
    each_crs(lambda core: send_last(me, core))
    arrived = last_rows.at[pl.ds(0, everyone - 1)]
    pltpu.make_async_copy(arrived, arrived, last_sem).wait()
    whole = jnp.broadcast_to(jnp.sum(last_rows[...], axis=0), (8, LANES)) / all_rows

    def final(d):
        return row_sum(jnp.where(lane_of == d * 4 + row_of, whole, 0.0))

    second_square = final(0)
    length_1 = jnp.sqrt(second_square / (start * start) + EPSILON)
    scale = 1.0 / (start * length_1)
    start_scale = 1.0 / start
    gram_11 = right_square * start_scale * start_scale
    gram_12 = final(1) * start_scale * scale
    gram_22 = second_square * scale * scale
    height_12 = final(2) * start_scale * scale
    height_22 = final(3) * scale * scale
    last_square = final(4) * scale * scale
    rest = (
        last_square
        - height_12 * height_12 * (2.0 - gram_11)
        - height_22 * height_22 * (2.0 - gram_22)
        + 2.0 * height_12 * height_22 * gram_12
    )
    length_2 = jnp.sqrt(jnp.maximum(rest, 0.0) + EPSILON)
    weights = least_squares(start, [[height_11, length_1], [height_12, height_22, length_2]])
    result = (weights[0] * start_scale) * first_z + (weights[1] * scale) * second_z
    following = (last * scale - (height_12 * start_scale) * right - (height_22 * scale) * second) / length_2
    for q in range(cols):
        both_ref[0, q] = result[q : q + 1]
        both_ref[1, q] = following[q : q + 1]

    for number in range(ROUNDS):
        gone = held[number].at[pl.ds(0, subs - 1)]
        pltpu.make_async_copy(gone, gone, send_sem).wait()
    for number in range(SHARES):
        gone = share.at[number, pl.ds(0, crs - 1)]
        pltpu.make_async_copy(gone, gone, share_send_sem).wait()
    pltpu.make_async_copy(arrived, arrived, last_send_sem).wait()


def body(
    right_side,
    own_block,
    coupling,
    local_inverse,
    coarse_basis,
    coarse_inverse,
    neighbours,
    margin_rows,
    block_counts,
):
    cols, rows = right_side.shape[0], right_side.shape[3]
    subs, crs = lax.axis_size("sub"), lax.axis_size("crs")
    kc = coarse_basis.shape[2]
    slots, block_rows = margin_rows.shape[2:]
    coarse_rows = crs * kc
    share_lanes = -(-coarse_rows // LANES) * LANES
    together = (LANES - 8) // kc
    groups = -(-subs // together)
    sizes = (subs, crs, cols, rows, kc, slots, share_lanes, together, groups)
    vmem = pl.BlockSpec(memory_space=pltpu.VMEM)
    stays = pl.BlockSpec(memory_space=pltpu.HBM)
    both = pl.pallas_call(
        functools.partial(kernel, sizes),
        out_shape=pltpu.VMEM((2, cols, 1, rows), WIDE),
        in_specs=[stays] * 9,
        out_specs=vmem,
        scratch_shapes=[
            pltpu.VMEM((cols, 1, rows), WIDE),
            pltpu.VMEM((rows, rows), LOW),
            pltpu.VMEM((rows, slots * block_rows), LOW),
            pltpu.VMEM((rows, rows + slots * block_rows), LOW),
            pltpu.VMEM((1, 1, kc, rows), WIDE),
            pltpu.VMEM((coarse_rows, subs * kc), LOW),
            pltpu.SMEM((1, 1, slots), jnp.int32),
            pltpu.VMEM((1, slots, 1, block_rows), jnp.int32),
            pltpu.SMEM((1, 1, 1), jnp.int32),
            pltpu.VMEM((ROUNDS, 16, LANES), LOW),
            *[pltpu.VMEM((subs, 16, LANES), LOW) for number in range(ROUNDS)],
            pltpu.VMEM((SHARES, crs, 8, share_lanes), WIDE),
            pltpu.VMEM((subs * crs, 1, LANES), WIDE),
            pltpu.VMEM((rows, rows), LOW),
            pltpu.VMEM((slots * block_rows, rows), LOW),
            pltpu.VMEM((rows + slots * block_rows, rows), LOW),
            pltpu.VMEM((rows, slots * block_rows), LOW),
            pltpu.VMEM((share_lanes, groups * LANES), LOW),
            pltpu.VMEM((LANES, rows), LOW),
            pltpu.VMEM((share_lanes, rows), WIDE),
            pltpu.VMEM((2 * share_lanes, rows), LOW),
            pltpu.SemaphoreType.DMA((9,)),
            pltpu.SemaphoreType.DMA,
            pltpu.SemaphoreType.DMA((ROUNDS,)),
            pltpu.SemaphoreType.DMA,
            pltpu.SemaphoreType.DMA((SHARES,)),
            pltpu.SemaphoreType.DMA,
            pltpu.SemaphoreType.DMA,
        ],
        compiler_params=pltpu.CompilerParams(
            collective_id=0, has_side_effects=True, vmem_limit_bytes=63 * 1024 * 1024
        ),
    )(
        right_side.reshape(cols, 1, rows),
        own_block.reshape(rows, -1),
        coupling.reshape(rows, -1),
        local_inverse.reshape(rows, -1),
        coarse_basis,
        coarse_inverse.reshape(coarse_rows, -1),
        neighbours,
        margin_rows.reshape(1, slots, 1, block_rows),
        block_counts.reshape(1, 1, 1),
    )
    shape = (cols, 1, 1, rows)
    return both[0].reshape(shape), both[1].reshape(shape)


def solution(mesh):
    in_specs = (
        P(None, "sub", "crs", None),
        P("sub", "crs", None, None),
        P("sub", "crs", None, None),
        P("sub", "crs", None, None),
        P("sub", "crs", None, None),
        P("sub", None, "crs", None),
        P("sub", "crs", None),
        P("sub", "crs", None, None),
        P("sub", "crs"),
    )
    out_specs = (P(None, "sub", "crs", None), P(None, "sub", "crs", None))
    return jax.shard_map(body, mesh=mesh, in_specs=in_specs, out_specs=out_specs, check_vma=False)
```

```python
import functools

import jax
import jax.numpy as jnp
from jax import lax
from jax.experimental import pallas as pl
from jax.experimental.pallas import tpu as pltpu
from jax.sharding import PartitionSpec as P

EPSILON = 1e-06
MESH = pl.DeviceIdType.MESH
LANES = 128
ROUNDS = 4
SHARES = 2
ORDER = (15, 7, 11, 3, 14, 6, 13, 5, 10, 2, 9, 1, 12, 4, 8)
AT = 120
NT = (((1,), (1,)), ((), ()))
LOW = jnp.bfloat16
WIDE = jnp.float32


def least_squares(start_norm, columns):
    cosines = []
    sine_terms = []
    triangle = []
    target = [start_norm] + [jnp.zeros_like(start_norm) for j in range(len(columns))]
    for j, column in enumerate(columns):
        column = list(column)
        for i in range(j):
            upper_value = cosines[i] * column[i] + sine_terms[i] * column[i + 1]
            column[i + 1] = -sine_terms[i] * column[i] + cosines[i] * column[i + 1]
            column[i] = upper_value
        radius = jnp.sqrt(column[j] * column[j] + column[j + 1] * column[j + 1])
        cosine = column[j] / radius
        sine_part = column[j + 1] / radius
        column[j] = radius
        target[j + 1] = -sine_part * target[j]
        target[j] = cosine * target[j]
        cosines.append(cosine)
        sine_terms.append(sine_part)
        triangle.append(column[: j + 1])
    weights = [None] * len(columns)
    for j in reversed(range(len(columns))):
        running = target[j]
        for k in range(j + 1, len(columns)):
            running = running - triangle[k][j] * weights[k]
        weights[j] = running / triangle[j][j]
    return weights


def kernel(
    sizes,
    right_hbm,
    own_hbm,
    couple_hbm,
    inverse_hbm,
    basis_hbm,
    coarse_hbm,
    listed_hbm,
    picked_hbm,
    counts_hbm,
    both_ref,
    right_ref,
    own_ref,
    couple_ref,
    inverse_ref,
    basis_ref,
    coarse_ref,
    listed_ref,
    picked_ref,
    counts_ref,
    sent,
    held_0,
    held_1,
    held_2,
    held_3,
    share,
    last_rows,
    own_t,
    couple_t,
    inverse_t,
    pick,
    coarse_wide,
    basis_parts,
    shifted,
    shifted_parts,
    load_sems,
    send_sem,
    recv_sems,
    share_send_sem,
    share_sems,
    last_send_sem,
    last_sem,
):
    subs, crs, cols, rows, kc, slots, share_lanes, together, groups = sizes
    held = (held_0, held_1, held_2, held_3)
    me = lax.axis_index("sub")
    mine = lax.axis_index("crs")
    all_rows = float(rows * subs * crs)
    row_of = lax.broadcasted_iota(jnp.int32, (8, LANES), 0)
    lane_of = lax.broadcasted_iota(jnp.int32, (8, LANES), 1)
    top = row_of < 4

    barrier = pltpu.get_barrier_semaphore()

    short = subs & (subs - 1) == 0 and subs <= 16

    def flipped(index, mask, bits):
        moved = index
        for k in range(bits):
            if mask >> k & 1:
                moved = moved + (1 << k) - (index // (1 << k)) % 2 * (2 << k)
        return moved

    def each_sub(act):
        if short:
            for mask in ORDER:
                if mask < subs:
                    act(flipped(me, mask, 4))
        else:

            def one(i, carry):
                act(lax.rem(me + i, subs))
                return carry

            lax.fori_loop(1, subs, one, 0)

    def each_crs(act):
        def one(i, carry):
            act(lax.rem(mine + i, crs))
            return carry

        if crs == 2:
            act(1 - mine)
        else:
            lax.fori_loop(1, crs, one, 0)

    def greet(sub, core):
        pl.semaphore_signal(barrier, inc=1, device_id=(sub, core), device_id_type=MESH)

    each_sub(lambda sub: greet(sub, mine))
    each_crs(lambda core: greet(me, core))

    pairs = [
        (right_hbm, right_ref),
        (basis_hbm, basis_ref),
        (picked_hbm, picked_ref),
        (counts_hbm, counts_ref),
        (coarse_hbm, coarse_ref),
        (listed_hbm, listed_ref),
        (inverse_hbm, inverse_ref),
        (own_hbm, own_ref),
        (couple_hbm, couple_ref),
    ]
    loads = [
        pltpu.make_async_copy(there, here, load_sems.at[n])
        for n, (there, here) in enumerate(pairs)
    ]
    for load in loads:
        load.start()

    def swap_halves(block):
        return pltpu.roll(block, 4, 0)

    def stack_parts(block):
        width = block.shape[1]
        high = block.astype(LOW).astype(WIDE)
        low = block - high
        at_top = lax.broadcasted_iota(jnp.int32, (8, width), 0) < 4
        return jnp.where(at_top, high, pltpu.roll(low, 4, 0)).astype(LOW)

    def nt(a, b):
        return lax.dot_general(a, b, NT, preferred_element_type=WIDE)

    def nn(a, b):
        return jnp.dot(a, b, preferred_element_type=WIDE)

    def turn(source, target):
        for k in range(0, source.shape[1], LANES):
            target[k : k + LANES, :] = source[:, k : k + LANES].T

    def row_sum(a):
        return jnp.sum(a, axis=1, keepdims=True)

    def restrict(block):
        both = nt(stack_parts(block), basis_parts[...])
        both = both + pltpu.roll(both, LANES // 2, 1)
        both = jnp.where(lane_of < kc, both + swap_halves(both), 0.0)
        moved = both
        for t in range(1, together):
            moved = jnp.where(lax.rem(me, together) == t, pltpu.roll(both, t * kc, 1), moved)
        return moved

    def encode(value):
        high = value.astype(LOW).astype(WIDE)
        rest = value - high
        middle = rest.astype(LOW).astype(WIDE)
        low = rest - middle
        spread = jnp.where(lane_of == AT, high, 0.0)
        spread = jnp.where(lane_of == AT + 1, middle, spread)
        return jnp.where(lane_of == AT + 2, low, spread)

    def pack(block, extra):
        first = jnp.where(top, block[:, :LANES], swap_halves(block[:, LANES : 2 * LANES]))
        second = jnp.where(top, block[:, 2 * LANES :], swap_halves(extra))
        return jnp.concatenate([first, second], axis=0).astype(LOW)

    def send(number, tile):
        sent[number] = tile

        def one(sub):
            pltpu.make_async_remote_copy(
                src_ref=sent.at[number],
                dst_ref=held[number].at[me],
                send_sem=send_sem,
                recv_sem=recv_sems.at[number],
                device_id=(sub, mine),
                device_id_type=MESH,
            ).start()

        each_sub(one)

    def receive(number):
        arrived = held[number].at[pl.ds(0, subs - 1)]
        pltpu.make_async_copy(arrived, arrived, recv_sems.at[number]).wait()

    def send_share(number, block):
        share[number, mine] = block

        def one(core):
            pltpu.make_async_remote_copy(
                src_ref=share.at[number, mine],
                dst_ref=share.at[number, mine],
                send_sem=share_send_sem,
                recv_sem=share_sems.at[number],
                device_id=(me, core),
                device_id_type=MESH,
            ).start()

        each_crs(one)

    def receive_share(number):
        arrived = share.at[number, pl.ds(0, crs - 1)]
        pltpu.make_async_copy(arrived, arrived, share_sems.at[number]).wait()
        total = share[number, 0]
        for c in range(1, crs):
            total = total + share[number, c]
        return total

    def fetch(number):
        lines = []
        for j in range(slots):
            tile = held[number][listed_ref[0, 0, j]].astype(WIDE)
            first = tile[:8]
            lines.append(jnp.concatenate([first, swap_halves(first), tile[8:]], axis=1))
        return nn(jnp.concatenate(lines, axis=0).astype(LOW), pick[...])

    def margin(fetched):
        parts = [
            fetched[8 * j : 8 * j + 8, LANES * j : LANES * j + LANES] for j in range(slots)
        ]
        return jnp.concatenate(parts, axis=1).astype(LOW)

    def group_sums(number):
        sums = []
        for g in range(groups):
            members = range(g * together, min(subs, (g + 1) * together))
            tiles = [held[number][s].astype(WIDE)[8:] for s in members]
            sums.append(functools.reduce(jnp.add, tiles))
        return sums

    def with_scalars(solved, totals):
        if share_lanes > LANES:
            totals = jnp.concatenate(
                [totals, jnp.zeros((8, share_lanes - LANES), WIDE)], axis=1
            )
        at_top = lax.broadcasted_iota(jnp.int32, (8, share_lanes), 0) < 4
        return jnp.where(at_top, pltpu.roll(solved, 4, 0), totals)

    def scalar(block):
        return row_sum(jnp.where((lane_of >= AT) & (lane_of < AT + 3), block, 0.0))

    def prolong(total):
        parts = stack_parts(total)
        both = nn(jnp.concatenate([parts, parts], axis=1), shifted_parts[...])
        return both + pltpu.roll(both, 4, 0)

    def precondition(number, share_number, own_part):
        receive(number)
        sums = group_sums(number)
        solved = nt(jnp.concatenate(sums, axis=1).astype(LOW), coarse_wide[...])
        fetched = fetch(number)
        totals = functools.reduce(jnp.add, sums)
        send_share(share_number, with_scalars(solved, totals))
        fine = own_part + nn(margin(fetched), inverse_t[rows:])
        total = receive_share(share_number)
        return fine + prolong(total), swap_halves(total[:, :LANES])

    loads[0].wait()
    loads[1].wait()
    right = jnp.concatenate(
        [right_ref[q] for q in range(cols)] + [jnp.zeros((8 - cols, rows), WIDE)], axis=0
    )
    basis = basis_ref[0, 0]
    basis_high = basis.astype(LOW).astype(WIDE)
    gap = jnp.zeros((LANES // 2 - kc, rows), WIDE)
    basis_parts[...] = jnp.concatenate(
        [basis_high, gap, basis - basis_high, gap], axis=0
    ).astype(LOW)
    extra = restrict(right) + encode(row_sum(right * right))
    tile = pack(right, extra)
    held_0[me] = tile
    pl.semaphore_wait(barrier, subs - 1 + crs - 1)
    send(0, tile)

    loads[2].wait()
    loads[3].wait()
    live = lax.broadcasted_iota(jnp.int32, (slots, LANES), 0) < counts_ref[0, 0, 0]
    wanted = jnp.where(
        live, jnp.concatenate([picked_ref[0, j] for j in range(slots)], axis=0), -1
    )
    row_index = lax.broadcasted_iota(jnp.int32, (rows, LANES), 0)
    for j in range(slots):
        pick[:, j * LANES : (j + 1) * LANES] = jnp.where(
            row_index == wanted[j : j + 1], 1.0, 0.0
        ).astype(LOW)
    shifted[...] = jnp.zeros_like(shifted)
    shifted[pl.ds(pl.multiple_of(mine * kc, 8), kc), :] = basis
    shifted_full = shifted[...]
    shifted_high = shifted_full.astype(LOW)
    shifted_parts[:share_lanes] = shifted_high
    shifted_parts[share_lanes:] = (shifted_full - shifted_high.astype(WIDE)).astype(LOW)
    loads[4].wait()
    coarse_rows = crs * kc
    coarse_cols = subs * kc
    coarse_wide[...] = jnp.zeros_like(coarse_wide)
    coarse_lane = lax.broadcasted_iota(jnp.int32, (coarse_rows, LANES), 1)
    for g in range(groups):
        first = g * together * kc
        count = min(together * kc, coarse_cols - first)
        base = first // LANES * LANES
        offset = first - base
        width = LANES if offset + count <= LANES else 2 * LANES
        window = coarse_ref[:, base : base + width].astype(WIDE)
        if offset:
            window = pltpu.roll(window, width - offset, 1)
        coarse_wide[:coarse_rows, g * LANES : (g + 1) * LANES] = jnp.where(
            coarse_lane < count, window[:, :LANES], 0.0
        ).astype(LOW)
    loads[5].wait()
    loads[6].wait()
    turn(inverse_ref, inverse_t)
    own_fine = nn(right.astype(LOW), inverse_t[:rows])

    first_z, totals = precondition(0, 0, own_fine)
    right_square = scalar(totals) / all_rows
    start = jnp.sqrt(right_square + EPSILON)

    nothing = jnp.zeros((8, LANES), WIDE)
    send(1, pack(first_z, nothing))
    loads[7].wait()
    loads[8].wait()
    turn(own_ref, own_t)
    turn(couple_ref, couple_t)
    own_part = nn(first_z.astype(LOW), own_t[...])
    receive(1)
    mapped = own_part + nn(margin(fetch(1)), couple_t[...])

    extra = restrict(mapped) + encode(row_sum(mapped * right))
    tile = pack(mapped, extra)
    held_2[me] = tile
    send(2, tile)
    own_fine = nn(mapped.astype(LOW), inverse_t[:rows])
    mapped_z, totals = precondition(2, 1, own_fine)
    height_11 = scalar(totals) / all_rows / (start * start)
    second_z = mapped_z - height_11 * first_z
    second = mapped - height_11 * right

    send(3, pack(second_z, nothing))
    own_part = nn(second_z.astype(LOW), own_t[...])
    products = [row_sum(second * second), row_sum(right * second)]
    receive(3)
    last = own_part + nn(margin(fetch(3)), couple_t[...])

    products = products + [row_sum(last * right), row_sum(last * second), row_sum(last * last)]
    line = jnp.zeros((8, LANES), WIDE)
    for d, value in enumerate(products):
        line = jnp.where((lane_of == d * 4 + row_of) & top, value, line)
    here = me * crs + mine
    everyone = subs * crs
    last_rows[here] = jnp.sum(line, axis=0, keepdims=True)

    def send_last(sub, core):
        pltpu.make_async_remote_copy(
            src_ref=last_rows.at[here],
            dst_ref=last_rows.at[here],
            send_sem=last_send_sem,
            recv_sem=last_sem,
            device_id=(sub, core),
            device_id_type=MESH,
        ).start()

    def send_last_to(sub):
        send_last(sub, mine)
        each_crs(lambda core: send_last(sub, core))

    each_sub(send_last_to)
    each_crs(lambda core: send_last(me, core))
    arrived = last_rows.at[pl.ds(0, everyone - 1)]
    pltpu.make_async_copy(arrived, arrived, last_sem).wait()
    whole = jnp.broadcast_to(jnp.sum(last_rows[...], axis=0), (8, LANES)) / all_rows

    def final(d):
        return row_sum(jnp.where(lane_of == d * 4 + row_of, whole, 0.0))

    second_square = final(0)
    length_1 = jnp.sqrt(second_square / (start * start) + EPSILON)
    scale = 1.0 / (start * length_1)
    start_scale = 1.0 / start
    gram_11 = right_square * start_scale * start_scale
    gram_12 = final(1) * start_scale * scale
    gram_22 = second_square * scale * scale
    height_12 = final(2) * start_scale * scale
    height_22 = final(3) * scale * scale
    last_square = final(4) * scale * scale
    rest = (
        last_square
        - height_12 * height_12 * (2.0 - gram_11)
        - height_22 * height_22 * (2.0 - gram_22)
        + 2.0 * height_12 * height_22 * gram_12
    )
    length_2 = jnp.sqrt(jnp.maximum(rest, 0.0) + EPSILON)
    weights = least_squares(start, [[height_11, length_1], [height_12, height_22, length_2]])
    result = (weights[0] * start_scale) * first_z + (weights[1] * scale) * second_z
    following = (last * scale - (height_12 * start_scale) * right - (height_22 * scale) * second) / length_2
    for q in range(cols):
        both_ref[0, q] = result[q : q + 1]
        both_ref[1, q] = following[q : q + 1]

    for number in range(ROUNDS):
        gone = held[number].at[pl.ds(0, subs - 1)]
        pltpu.make_async_copy(gone, gone, send_sem).wait()
    for number in range(SHARES):
        gone = share.at[number, pl.ds(0, crs - 1)]
        pltpu.make_async_copy(gone, gone, share_send_sem).wait()
    pltpu.make_async_copy(arrived, arrived, last_send_sem).wait()


def body(
    right_side,
    own_block,
    coupling,
    local_inverse,
    coarse_basis,
    coarse_inverse,
    neighbours,
    margin_rows,
    block_counts,
):
    cols, rows = right_side.shape[0], right_side.shape[3]
    subs, crs = lax.axis_size("sub"), lax.axis_size("crs")
    kc = coarse_basis.shape[2]
    slots, block_rows = margin_rows.shape[2:]
    coarse_rows = crs * kc
    share_lanes = -(-coarse_rows // LANES) * LANES
    together = (LANES - 8) // kc
    groups = -(-subs // together)
    sizes = (subs, crs, cols, rows, kc, slots, share_lanes, together, groups)
    vmem = pl.BlockSpec(memory_space=pltpu.VMEM)
    stays = pl.BlockSpec(memory_space=pltpu.HBM)
    both = pl.pallas_call(
        functools.partial(kernel, sizes),
        out_shape=pltpu.VMEM((2, cols, 1, rows), WIDE),
        in_specs=[stays] * 9,
        out_specs=vmem,
        scratch_shapes=[
            pltpu.VMEM((cols, 1, rows), WIDE),
            pltpu.VMEM((rows, rows), LOW),
            pltpu.VMEM((rows, slots * block_rows), LOW),
            pltpu.VMEM((rows, rows + slots * block_rows), LOW),
            pltpu.VMEM((1, 1, kc, rows), WIDE),
            pltpu.VMEM((coarse_rows, subs * kc), LOW),
            pltpu.SMEM((1, 1, slots), jnp.int32),
            pltpu.VMEM((1, slots, 1, block_rows), jnp.int32),
            pltpu.SMEM((1, 1, 1), jnp.int32),
            pltpu.VMEM((ROUNDS, 16, LANES), LOW),
            *[pltpu.VMEM((subs, 16, LANES), LOW) for number in range(ROUNDS)],
            pltpu.VMEM((SHARES, crs, 8, share_lanes), WIDE),
            pltpu.VMEM((subs * crs, 1, LANES), WIDE),
            pltpu.VMEM((rows, rows), LOW),
            pltpu.VMEM((slots * block_rows, rows), LOW),
            pltpu.VMEM((rows + slots * block_rows, rows), LOW),
            pltpu.VMEM((rows, slots * block_rows), LOW),
            pltpu.VMEM((share_lanes, groups * LANES), LOW),
            pltpu.VMEM((LANES, rows), LOW),
            pltpu.VMEM((share_lanes, rows), WIDE),
            pltpu.VMEM((2 * share_lanes, rows), LOW),
            pltpu.SemaphoreType.DMA((9,)),
            pltpu.SemaphoreType.DMA,
            pltpu.SemaphoreType.DMA((ROUNDS,)),
            pltpu.SemaphoreType.DMA,
            pltpu.SemaphoreType.DMA((SHARES,)),
            pltpu.SemaphoreType.DMA,
            pltpu.SemaphoreType.DMA,
        ],
        compiler_params=pltpu.CompilerParams(
            collective_id=0, has_side_effects=True, vmem_limit_bytes=63 * 1024 * 1024
        ),
    )(
        right_side.reshape(cols, 1, rows),
        own_block.reshape(rows, -1),
        coupling.reshape(rows, -1),
        local_inverse.reshape(rows, -1),
        coarse_basis,
        coarse_inverse.reshape(coarse_rows, -1),
        neighbours,
        margin_rows.reshape(1, slots, 1, block_rows),
        block_counts.reshape(1, 1, 1),
    )
    shape = (cols, 1, 1, rows)
    return both[0].reshape(shape), both[1].reshape(shape)


def solution(mesh):
    in_specs = (
        P(None, "sub", "crs", None),
        P("sub", "crs", None, None),
        P("sub", "crs", None, None),
        P("sub", "crs", None, None),
        P("sub", "crs", None, None),
        P("sub", None, "crs", None),
        P("sub", "crs", None),
        P("sub", "crs", None, None),
        P("sub", "crs"),
    )
    out_specs = (P(None, "sub", "crs", None), P(None, "sub", "crs", None))
    return jax.shard_map(body, mesh=mesh, in_specs=in_specs, out_specs=out_specs, check_vma=False)
```
